32 devices in a mesh: dp: 2 (over x), graph: 16 (over z, y, core).
Axes of the slice: x: 2, y: 2, z: 4, core: 2. Of those that a mesh axis runs over, the one named last changes fastest.
Arguments:
- node_feats: bfloat16 [2, 128, 25, 128], P('dp', 'graph'), may hold values from -6 to 6
- node_cot: bfloat16 [2, 128, 25, 128], P('dp', 'graph'), may hold values from -6 to 6
- wigner: bfloat16 [2, 19, 25, 4096], P('dp', None, None, 'graph'), may hold values from -4 to 4, as said below
- radial: bfloat16 [2, 4096, 128], P('dp', 'graph'), may hold values from 0.049804688 to 0.5
- source_atom: int32 [2, 4096], P('dp', 'graph'), may hold values from 0 to 127, as said below
- target_index: int32 [2, 4096], P('dp', 'graph'), may hold values from 0 to 7
- edge_counts: int32 [2, 16], P('dp', 'graph'), may hold values from 128 to 256
- merged_weights: bfloat16 [2, 1228800], P('dp', 'graph'), may hold values from -0.25 to 0.25
- mixing: float32 [2, 32], replicated, may hold values from 0.005 to 0.2
Outputs:
- atom_grads: float32 [2, 128, 25, 128], P('dp', 'graph')
- expert_grads: float32 [32, 1228800], P('dp', 'graph')
The draws below stay inside these ranges and needn't reach their ends.
Inputs may be any that keep to these rules, and one draw needn't show every extreme that they name: `source_atom`: an edge slot held by shard q has its source among the atoms of shards q - 1, q and q + 1 of its system: indices from 8 * max(q - 1, 0) to 8 * min(q + 2, 16) - 1. `edge_counts`: slots of a shard from its count on are padding. `wigner`: an entry is zero where the degree of its frame row differs from the degree of its node coefficient.
All inputs are finite; a program needn't handle non-finite values.
Results may differ from the reference program's by a relative error of at most 0.005.
Values may be sent and summed in bfloat16 or wider, within the bound.
No kernel may reach another device: no remote copies, remote signals or barrier semaphores. Data moves between devices by JAX's collectives and lax.ppermute only.
A program may use at most 128 MiB of HBM per device.

```python
import math
import jax
import jax.numpy as jnp
import numpy as np
from jax import lax

CHANNELS = 128
EXPERTS = 32
COEFS = 25
FRAME = 19
EDGES_DEV = 256
ATOMS_DEV = 8
SHARDS = 16
SYSTEMS = 2
ATOMS = 128
EDGES = 4096
PARAMS = 1228800


def degree_scaling():
    row_degrees = np.array([0, 1, 2, 3, 4, 1, 2, 3, 4, 1, 2, 3, 4, 2, 3, 4, 2, 3, 4], dtype=np.float32)
    col_degrees = np.array([degree for degree in range(5) for repeat in range(2 * degree + 1)], dtype=np.float32)
    matches = (row_degrees[:, None] == col_degrees[None, :]).astype(np.float32)
    return matches / np.sqrt(2.0 * row_degrees[:, None] + 1.0)


def draw_wigner(key, part):
    scaling = jnp.asarray(degree_scaling())
    values = jax.random.normal(jax.random.fold_in(key, 11), (SYSTEMS, FRAME, COEFS, EDGES), jnp.float32)
    values = jnp.clip(values, -4.0, 4.0)
    return (values * scaling[None, :, :, None]).astype(jnp.bfloat16)


def draw_source_atom(key, part):
    edge_ids = jnp.arange(EDGES, dtype=jnp.int32)
    shard_ids = edge_ids // EDGES_DEV
    lowest = jnp.maximum(shard_ids - 1, 0) * ATOMS_DEV
    highest = jnp.minimum(shard_ids + 2, SHARDS) * ATOMS_DEV
    drawn = jax.random.randint(jax.random.fold_in(key, 12), (SYSTEMS, EDGES), 0, 1 << 24, jnp.int32)
    return (lowest[None, :] + drawn % (highest - lowest)[None, :]).astype(jnp.int32)


def touch_ends(values, key, smallest, top_value):
    longest = values.shape.index(max(values.shape))
    spots = []
    for shift in (0, 1):
        where = [jax.random.randint(jax.random.fold_in(key, axis), (), 0, length) for axis, length in enumerate(values.shape)]
        where[longest] = (where[longest] + shift) % values.shape[longest]
        spots.append(tuple(where))
    return values.at[spots[0]].set(smallest).at[spots[1]].set(top_value)


def block_scale(key, shape, cuts, least, top_value):
    def one(dim, shards_of):
        steps = jax.random.uniform(jax.random.fold_in(jax.random.fold_in(key, 6), dim), (shards_of,), jnp.float32, least / len(cuts), top_value / len(cuts))
        return jnp.repeat(jnp.exp(steps), shape[dim] // shards_of).reshape((-1,) + (1,) * (len(shape) - dim - 1))

    gain = one(*cuts[0])
    for cut in cuts[1:]:
        gain = gain * one(*cut)
    return gain


def bell_draw(stream_key, shape, width, reach, pieces=(), kind=jnp.bfloat16):
    gain = block_scale(stream_key, shape, pieces, -0.22, 0.18) if pieces else 1.0
    values = jax.random.normal(stream_key, shape, jnp.float32) * width * gain
    return jnp.minimum(jnp.maximum(values, -reach), reach).astype(kind)


def setup_inputs(seed: int = 0) -> dict:
    streams_of = jax.random.split(jax.random.key(seed), 10)
    return {
        "node_feats": bell_draw(streams_of[0], (SYSTEMS, ATOMS, COEFS, CHANNELS), 1.0, 6.0, ((0, 2), (1, 16))),
        "node_cot": bell_draw(streams_of[1], (SYSTEMS, ATOMS, COEFS, CHANNELS), 1.0, 6.0, ((0, 2), (1, 16))),
        "wigner": draw_wigner(jax.random.fold_in(streams_of[9], 71), 0),
        "radial": jnp.clip(jnp.exp(math.log(0.5) - 2.306499 * jax.random.uniform(streams_of[3], (SYSTEMS, EDGES, CHANNELS), jnp.float32) ** block_scale(streams_of[3], (SYSTEMS, EDGES, CHANNELS), ((0, 2), (1, 16)), -0.2, 0.2)), 0.049804688, 0.5).astype(jnp.bfloat16),
        "source_atom": draw_source_atom(jax.random.fold_in(streams_of[9], 71), 0),
        "target_index": touch_ends(jax.random.randint(streams_of[5], (SYSTEMS, EDGES), 0, ATOMS_DEV), jax.random.fold_in(streams_of[5], 1), 0, ATOMS_DEV - 1).astype(jnp.int32),
        "edge_counts": touch_ends(jax.random.randint(streams_of[6], (SYSTEMS, SHARDS), EDGES_DEV // 2, EDGES_DEV + 1), jax.random.fold_in(streams_of[6], 1), EDGES_DEV // 2, EDGES_DEV).astype(jnp.int32),
        "merged_weights": bell_draw(streams_of[7], (SYSTEMS, PARAMS), (4 * CHANNELS) ** -0.5, 0.25, ((0, 2), (1, 16))),
        "mixing": jnp.clip(jnp.exp(jax.random.uniform(streams_of[8], (SYSTEMS, EXPERTS), jnp.float32, math.log(0.005), math.log(0.2))), 0.005, 0.2),
    }


def split_groups(frame_rows):
    edge_rows = frame_rows.shape[0]
    channels = frame_rows.shape[2]
    bounds = ((0, 5), (5, 9), (9, 13), (13, 16), (16, 19))
    return [frame_rows[:, lower_row:upper_row].reshape(edge_rows, (upper_row - lower_row) * channels) for lower_row, upper_row in bounds]


def unpack_weights(flat_weights, channels):
    weight_blocks = []
    offset_entry = 0
    for group_rows in (5, 4, 4, 3, 3):
        extent = group_rows * channels
        weight_blocks.append(flat_weights[offset_entry:offset_entry + extent * extent].reshape(extent, extent))
        offset_entry = offset_entry + extent * extent
    return weight_blocks


def contract_rows(left_side, right_side):
    return lax.dot_general(left_side, right_side, (((0,), (0,)), ((), ())), preferred_element_type=jnp.float32)


def times_transposed(left_side, right_side):
    return lax.dot_general(left_side, right_side, (((1,), (1,)), ((), ())), preferred_element_type=jnp.float32)


def so2_backward(weight_blocks, rotated, frame_cot):
    inputs = split_groups(rotated)
    upstream = split_groups(frame_cot)
    grads = [contract_rows(inputs[0], upstream[0])]
    backs = [times_transposed(upstream[0], weight_blocks[0])]
    for group_first in (1, 3):
        in_plus = inputs[group_first]
        in_minus = inputs[group_first + 1]
        up_plus = upstream[group_first]
        up_minus = upstream[group_first + 1]
        w_real = weight_blocks[group_first]
        w_imag = weight_blocks[group_first + 1]
        grads.append(contract_rows(jnp.concatenate([in_plus, in_minus], 0), jnp.concatenate([up_plus, up_minus], 0)))
        grads.append(contract_rows(jnp.concatenate([in_plus, -in_minus], 0), jnp.concatenate([up_minus, up_plus], 0)))
        backs.append(times_transposed(up_plus, w_real) + times_transposed(up_minus, w_imag))
        backs.append(times_transposed(up_minus, w_real) - times_transposed(up_plus, w_imag))
    edge_rows = rotated.shape[0]
    channels = rotated.shape[2]
    flat_grad = jnp.concatenate([piece.reshape(-1) for piece in grads])
    back_rows = jnp.concatenate([piece.reshape(edge_rows, -1, channels) for piece in backs], 1)
    return flat_grad, back_rows


def reference(node_feats, node_cot, wigner, radial, source_atom, target_index, edge_counts, merged_weights, mixing):
    channels = node_feats.shape[3]

    def one_system(system_args):
        feats, cotangent, rotation, radial_rows, sources, targets, counts, flat_weights = system_args
        weight_blocks = unpack_weights(flat_weights, channels)

        def shard_step(carried, shard_index):
            weight_total, atom_total = carried
            first_edge = shard_index * EDGES_DEV
            rot_block = lax.dynamic_slice_in_dim(rotation, first_edge, EDGES_DEV, 2).astype(jnp.float32)
            source_block = lax.dynamic_slice_in_dim(sources, first_edge, EDGES_DEV, 0)
            target_block = lax.dynamic_slice_in_dim(targets, first_edge, EDGES_DEV, 0) + shard_index * ATOMS_DEV
            radial_block = lax.dynamic_slice_in_dim(radial_rows, first_edge, EDGES_DEV, 0).astype(jnp.float32)
            live_rows = (jnp.arange(EDGES_DEV, dtype=jnp.int32) < counts[shard_index]).astype(jnp.bfloat16)
            src_feats = jnp.take(feats, source_block, axis=0)
            rotated = (jnp.einsum("ije,ejc->eic", rot_block, src_feats.astype(jnp.float32)) * radial_block[:, None, :]).astype(jnp.bfloat16)
            edge_cot = jnp.take(cotangent, target_block, axis=0) * live_rows[:, None, None]
            frame_cot = jnp.einsum("ije,ejc->eic", rot_block, edge_cot.astype(jnp.float32)).astype(jnp.bfloat16)
            flat_grad, back_rows = so2_backward(weight_blocks, rotated, frame_cot)
            rot_cot = (back_rows * radial_block[:, None, :]).astype(jnp.bfloat16)
            edge_src_cot = jnp.einsum("ije,eic->ejc", rot_block, rot_cot.astype(jnp.float32))
            atom_total = atom_total + jax.ops.segment_sum(edge_src_cot, source_block, num_segments=ATOMS)
            return (weight_total + flat_grad, atom_total), None

        initial = (jnp.zeros((PARAMS,), jnp.float32), jnp.zeros((ATOMS, COEFS, channels), jnp.float32))
        (weight_total, atom_total), unused = lax.scan(shard_step, initial, jnp.arange(SHARDS, dtype=jnp.int32))
        return weight_total, atom_total

    weight_grad, atom_grads = lax.map(one_system, (node_feats, node_cot, wigner, radial, source_atom, target_index, edge_counts, merged_weights))
    expert_grads = lax.dot_general(mixing, weight_grad, (((0,), (0,)), ((), ())), precision=lax.Precision.HIGHEST, preferred_element_type=jnp.float32)
    return atom_grads, expert_grads
```

```python
import functools

import jax
import jax.numpy as jnp
from jax import lax
from jax.experimental import pallas as pl
from jax.experimental.pallas import tpu as pltpu
from jax.sharding import PartitionSpec as P

BF16 = jnp.bfloat16
F32 = jnp.float32
LANES = 128
GROUPS = ((0, 5), (5, 9), (9, 13), (13, 16), (16, 19))
FRAME_ROWS = tuple(
    tuple(
        first + degree - order
        for first, order in ((0, 0), (5, 1), (9, 1), (13, 2), (16, 2))
        if degree >= order
    )
    for degree in range(5)
)
NODE_COLS = tuple(tuple(range(l * l, (l + 1) * (l + 1))) for l in range(5))
WEIGHTS = (5, 4, 4, 3, 3)


def first_rows():
    rows, out = 0, []
    for group_rows in WEIGHTS:
        out.append(rows)
        rows += group_rows * group_rows * LANES
    return out


def place(row):
    if row < 5:
        return 0, row, 0
    if row < 13:
        return 1, (row - 5) % 4, (row - 5) // 4
    return 2, (row - 13) % 3, (row - 13) // 3


def for_chunks(channels, edges, size, body):
    for edge_first in range(0, edges, LANES):

        def step(turn, unused, edge_first=edge_first):
            body(pl.multiple_of(turn * size, size), edge_first)
            return unused

        lax.fori_loop(0, channels // size, step, 0)


def nt(left, right):
    return lax.dot_general(left, right, (((1,), (1,)), ((), ())), preferred_element_type=F32)


def tn(left, right):
    return lax.dot_general(left, right, (((0,), (0,)), ((), ())), preferred_element_type=F32)


def forward_kernel(
    info, source, target, feats_up, feats_own, feats_down, cot, wigner, radial,
    b0, b1, b1i, b2, b2i, keep, send,
    rot, gate, flat, picked, a0, a1, a2, grad,
):
    atoms, coefs, channels = feats_own.shape
    edges = source.shape[1]
    rot[...] = wigner[...].astype(F32)
    gate[...] = radial[...].astype(F32).T
    amat = (a0, a1, a2)
    bmat = (b0, b1, b2)
    bimag = (None, b1i, b2i)
    pitch = flat.shape[0] // (3 * atoms)

    def gather(pieces, pick):
        for place_of, piece in enumerate(pieces):
            for atom in range(atoms):
                at = (place_of * atoms + atom) * pitch
                flat[at : at + coefs, :] = piece[atom].astype(F32)
        count = len(pieces) * atoms
        for coef in range(coefs):
            block = flat[pl.ds(coef, count, stride=pitch), :].astype(BF16)
            picked[coef] = tn(block, pick)

    def rotate(emit):
        def body(at, edge_first):
            lanes = slice(edge_first, edge_first + LANES)
            for rows, cols in zip(FRAME_ROWS, NODE_COLS):
                totals = [None] * len(rows)
                for col in cols:
                    value = picked[col, pl.ds(at, 32), lanes]
                    for n, row in enumerate(rows):
                        term = rot[row, col : col + 1, lanes] * value
                        totals[n] = term if totals[n] is None else totals[n] + term
                for row, total in zip(rows, totals):
                    emit(row, at, edge_first, total)

        for_chunks(channels, edges, 32, body)

    live = lax.broadcasted_iota(jnp.int32, (1, edges), 1) < info[1]
    wanted = jnp.where(live, target[...], -1)
    pick = lax.broadcasted_iota(jnp.int32, (atoms, edges), 0) == wanted
    gather((cot,), pick.astype(F32).astype(BF16))

    def emit_b(row, at, edge_first, total):
        which, block, half = place(row)
        rows = pl.ds(pl.multiple_of(block * channels + at, 32), 32)
        value = total.astype(BF16)
        lanes = slice(half * edges + edge_first, half * edges + edge_first + LANES)
        bmat[which][rows, lanes] = value
        if which:
            other = 1 - half
            lanes = slice(other * edges + edge_first, other * edges + edge_first + LANES)
            bimag[which][rows, lanes] = value if half else (-total).astype(BF16)

    rotate(emit_b)

    nearest = source[...] - (info[0] - 1) * atoms
    pick = lax.broadcasted_iota(jnp.int32, (3 * atoms, edges), 0) == nearest
    gather((feats_up, feats_own, feats_down), pick.astype(F32).astype(BF16))

    def emit_a(row, at, edge_first, total):
        which, block, half = place(row)
        rows = pl.ds(pl.multiple_of(block * channels + at, 32), 32)
        gated = total * gate[pl.ds(at, 32), edge_first : edge_first + LANES]
        lanes = slice(half * edges + edge_first, half * edges + edge_first + LANES)
        amat[which][rows, lanes] = gated.astype(BF16)

    rotate(emit_a)

    rights = (b0, b1, b1i, b2, b2i)
    lefts = (a0, a1, a1, a2, a2)
    for left, right, blocks, first in zip(lefts, rights, WEIGHTS, first_rows()):
        extent = blocks * LANES
        for block in range(0, blocks, 2):
            width = min(2, blocks - block)
            product = nt(left[...], right[block * LANES : (block + width) * LANES, :])
            for n in range(width):
                grad[pl.ds(first + block + n, extent, stride=blocks), :] = product[
                    :, n * LANES : (n + 1) * LANES
                ]
    shards, rows = keep.shape[0], keep.shape[1]
    parity = lax.rem(info[0], 2)
    for n in range(shards):
        keep[n] = grad[pl.ds((2 * n + parity) * rows, rows), :]
        send[n] = grad[pl.ds((2 * n + 1 - parity) * rows, rows), :].astype(BF16)


def backward_kernel(
    info, source, weights, b0, b1, b1i, b2, b2i, wigner, radial,
    out,
    rot, gate, flat, w0, w1r, w1i, w2r, w2i, back, spread,
):
    parts, atoms, coefs, channels = out.shape
    edges = source.shape[1]
    shards, shard_rows = weights.shape[0], weights.shape[1]
    rot[...] = wigner[...].astype(F32)
    gate[...] = radial[...].astype(F32).T
    for n in range(shards):
        flat[n * shard_rows : (n + 1) * shard_rows, :] = weights[n].astype(F32)
    for matrix, blocks, first in zip((w0, w1r, w1i, w2r, w2i), WEIGHTS, first_rows()):
        for block in range(blocks):
            matrix[:, block * LANES : (block + 1) * LANES] = flat[
                pl.ds(first + block, blocks * LANES, stride=blocks), :
            ].astype(BF16)

    dot = functools.partial(jnp.dot, preferred_element_type=F32)
    for row in range(5):
        rows = slice(row * channels, (row + 1) * channels)
        back[row] = dot(w0[rows, :], b0[...]) * gate[...]
    for first, real, imag, upper, lower, blocks in (
        (5, w1r, w1i, b1, b1i, 4),
        (13, w2r, w2i, b2, b2i, 3),
    ):
        for block in range(blocks):
            rows = slice(block * channels, (block + 1) * channels)
            both = dot(real[rows, :], upper[...]) + dot(imag[rows, :], lower[...])
            back[first + block] = both[:, :edges] * gate[...]
            back[first + blocks + block] = both[:, edges:] * gate[...]

    def body(at, edge_first):
        lanes = slice(edge_first, edge_first + LANES)
        for rows, cols in zip(FRAME_ROWS, NODE_COLS):
            totals = [None] * len(cols)
            for row in rows:
                value = back[row, pl.ds(at, 16), lanes]
                for n, col in enumerate(cols):
                    term = rot[row, col : col + 1, lanes] * value
                    totals[n] = term if totals[n] is None else totals[n] + term
            for col, total in zip(cols, totals):
                spread[col, pl.ds(at, 16), lanes] = total.astype(BF16)

    for_chunks(channels, edges, 16, body)
    nearest = source[...] - (info[0] - 1) * atoms
    pick = lax.broadcasted_iota(jnp.int32, (3 * atoms, edges), 0) == nearest
    pick = pick.astype(F32).astype(BF16)
    for col in range(coefs):
        out[:, :, col, :] = nt(pick, spread[col]).reshape(parts, atoms, channels)


def expert_kernel(columns, own_rows, *refs):
    others, out = refs[:-1], refs[-1]
    experts = out.shape[0]
    rows = own_rows.shape[0]
    systems = 1 + len(others)
    scales = [
        jnp.broadcast_to(columns[s], (experts, LANES)) for s in range(systems)
    ]
    group = 12

    def step(turn, unused):
        for n in range(group):
            row = turn * group + n
            total = own_rows[pl.ds(row, 1), :] * scales[0]
            for other, scale in zip(others, scales[1:]):
                total = total + other[pl.ds(row, 1), :] * scale
            out[:, pl.ds(pl.multiple_of(row * LANES, LANES), LANES)] = total
        return unused

    lax.fori_loop(0, rows // group, step, 0)


def spec(space=pltpu.VMEM):
    return pl.BlockSpec(memory_space=space)


PARAMS = pltpu.CompilerParams(vmem_limit_bytes=56 * 1024 * 1024)


def swap(x, axis, bit):
    size = lax.axis_size(axis)
    return lax.ppermute(x, axis, [(i, i ^ bit) for i in range(size)])


def on_device(
    node_feats, node_cot, wigner, radial, source_atom, target_index, edge_counts,
    merged_weights, mixing,
):
    atoms, coefs, channels = node_feats.shape[1:]
    edges = source_atom.shape[1]
    size = lax.axis_size("graph")
    bits = size.bit_length() - 1
    index = lax.axis_index("graph")
    shard_rows = merged_weights.shape[1] // LANES
    total_rows = shard_rows * size

    feats = node_feats[0]
    feats_up = lax.ppermute(feats, "graph", [(i, i + 1) for i in range(size - 1)])
    feats_down = lax.ppermute(feats, "graph", [(i + 1, i) for i in range(size - 1)])

    gathered = merged_weights.reshape(1, shard_rows, LANES)
    for bit in reversed(range(bits)):
        other = swap(gathered, "graph", 1 << bit)
        mine = ((index >> bit) & 1) == 0
        low = jnp.where(mine, gathered, other)
        high = jnp.where(mine, other, gathered)
        gathered = jnp.stack([low, high], axis=1).reshape(-1, shard_rows, LANES)

    info = jnp.stack([index.astype(jnp.int32), edge_counts[0, 0]])
    shapes = [(5, 1), (4, 2), (4, 2), (3, 2), (3, 2)]
    half = size // 2
    smem = spec(pltpu.SMEM)
    outs = pl.pallas_call(
        forward_kernel,
        out_shape=[
            jax.ShapeDtypeStruct((g * channels, h * edges), BF16) for g, h in shapes
        ]
        + [
            jax.ShapeDtypeStruct((half, shard_rows, LANES), F32),
            jax.ShapeDtypeStruct((half, shard_rows, LANES), BF16),
        ],
        in_specs=[smem] + [spec()] * 8,
        out_specs=[spec()] * 7,
        scratch_shapes=[
            pltpu.VMEM((19, coefs, edges), F32),
            pltpu.VMEM((channels, edges), F32),
            pltpu.VMEM((3 * atoms * 32, channels), F32),
            pltpu.VMEM((coefs, channels, edges), F32),
            pltpu.VMEM((5 * channels, edges), BF16),
            pltpu.VMEM((4 * channels, 2 * edges), BF16),
            pltpu.VMEM((3 * channels, 2 * edges), BF16),
            pltpu.VMEM((total_rows, LANES), F32),
        ],
        compiler_params=PARAMS,
        cost_estimate=pl.CostEstimate(
            flops=3 * 10**9, bytes_accessed=10 * 10**6, transcendentals=0
        ),
        name="forward",
    )(
        info, source_atom, target_index, feats_up, feats, feats_down, node_cot[0],
        wigner[0], radial[0],
    )
    bmats, keep, send = outs[:5], outs[5], outs[6]

    total = keep + swap(send, "graph", 1).astype(F32)
    for bit in range(1, bits):
        total = total.reshape(-1, 2, shard_rows, LANES)
        side = (index >> bit) & 1
        away = lax.dynamic_index_in_dim(total, 1 - side, 1, keepdims=False)
        stay = lax.dynamic_index_in_dim(total, side, 1, keepdims=False)
        total = stay + swap(away.astype(BF16), "graph", 1 << bit).astype(F32)
    share = total[0]

    systems = lax.axis_size("dp")
    place_dp = lax.axis_index("dp")
    rounded = share.astype(BF16)
    others = [
        lax.ppermute(rounded, "dp", [(i, (i + n) % systems) for i in range(systems)])
        .astype(F32)
        for n in range(1, systems)
    ]
    own_experts = mixing.shape[1] // systems
    columns = lax.dynamic_slice_in_dim(mixing, place_dp * own_experts, own_experts, 1)
    order = jnp.stack([(place_dp - n) % systems for n in range(systems)])
    columns = jnp.take(columns, order, axis=0)[:, :, None]
    expert_part = pl.pallas_call(
        expert_kernel,
        out_shape=jax.ShapeDtypeStruct((own_experts, shard_rows * LANES), F32),
        in_specs=[spec()] * (1 + systems),
        out_specs=spec(),
        compiler_params=PARAMS,
        cost_estimate=pl.CostEstimate(
            flops=5 * 10**6, bytes_accessed=6 * 10**6, transcendentals=0
        ),
        name="experts",
    )(columns, share, *others)

    atom_total = pl.pallas_call(
        backward_kernel,
        out_shape=jax.ShapeDtypeStruct((3, atoms, coefs, channels), F32),
        in_specs=[smem] + [spec()] * 9,
        out_specs=spec(),
        scratch_shapes=[
            pltpu.VMEM((19, coefs, edges), F32),
            pltpu.VMEM((channels, edges), F32),
            pltpu.VMEM((total_rows, LANES), F32),
        ]
        + [pltpu.VMEM((g * channels, g * channels), BF16) for g in WEIGHTS]
        + [
            pltpu.VMEM((19, channels, edges), F32),
            pltpu.VMEM((coefs, channels, edges), BF16),
        ],
        compiler_params=PARAMS,
        cost_estimate=pl.CostEstimate(
            flops=3 * 10**9, bytes_accessed=10 * 10**6, transcendentals=0
        ),
        name="backward",
    )(info, source_atom, gathered, *bmats, wigner[0], radial[0])
    from_up = lax.ppermute(atom_total[2], "graph", [(i, i + 1) for i in range(size - 1)])
    from_down = lax.ppermute(atom_total[0], "graph", [(i + 1, i) for i in range(size - 1)])
    atom_grads = (atom_total[1] + from_up + from_down)[None]
    return (atom_grads, expert_part)


def solution(mesh):
    in_specs = (
        P("dp", "graph", None, None),
        P("dp", "graph", None, None),
        P("dp", None, None, "graph"),
        P("dp", "graph", None),
        P("dp", "graph"),
        P("dp", "graph"),
        P("dp", "graph"),
        P("dp", "graph"),
        P(),
    )
    out_specs = (P("dp", "graph", None, None), P("dp", "graph"))
    return jax.shard_map(
        on_device, mesh=mesh, in_specs=in_specs, out_specs=out_specs, check_vma=False
    )
```

```python
import functools

import jax
import jax.numpy as jnp
from jax import lax
from jax.experimental import pallas as pl
from jax.experimental.pallas import tpu as pltpu
from jax.sharding import PartitionSpec as P

BF16 = jnp.bfloat16
F32 = jnp.float32
LANES = 128
GROUPS = ((0, 5), (5, 9), (9, 13), (13, 16), (16, 19))
FRAME_ROWS = tuple(
    tuple(
        first + degree - order
        for first, order in ((0, 0), (5, 1), (9, 1), (13, 2), (16, 2))
        if degree >= order
    )
    for degree in range(5)
)
NODE_COLS = tuple(tuple(range(l * l, (l + 1) * (l + 1))) for l in range(5))
WEIGHTS = (5, 4, 4, 3, 3)


def first_rows():
    rows, out = 0, []
    for group_rows in WEIGHTS:
        out.append(rows)
        rows += group_rows * group_rows * LANES
    return out


def place(row):
    if row < 5:
        return 0, row, 0
    if row < 13:
        return 1, (row - 5) % 4, (row - 5) // 4
    return 2, (row - 13) % 3, (row - 13) // 3


def for_chunks(channels, edges, size, body):
    for edge_first in range(0, edges, LANES):

        def step(turn, unused, edge_first=edge_first):
            body(pl.multiple_of(turn * size, size), edge_first)
            return unused

        lax.fori_loop(0, channels // size, step, 0)


def nt(left, right):
    return lax.dot_general(left, right, (((1,), (1,)), ((), ())), preferred_element_type=F32)


def tn(left, right):
    return lax.dot_general(left, right, (((0,), (0,)), ((), ())), preferred_element_type=F32)


def one_hot(count, wanted):
    edges = wanted.shape[1]
    hit = lax.broadcasted_iota(jnp.int32, (count, edges), 0) == wanted
    return hit.astype(F32).astype(BF16)


def near_pick(source, atoms):
    index = lax.axis_index("graph")
    shard = lax.div(source[...], atoms)
    slot = jnp.where(shard == index, 1, jnp.where(shard == (index ^ 1), 0, 2))
    return one_hot(3 * atoms, (slot - shard) * atoms + source[...])


def gather(pieces, pick, picked):
    for coef in range(picked.shape[0]):
        parts = [piece[coef].astype(F32) for piece in pieces]
        block = parts[0] if len(parts) == 1 else jnp.concatenate(parts, axis=0)
        picked[coef] = tn(block.astype(BF16), pick)


def rotate(rot, picked, emit):
    channels, edges = picked.shape[1:]

    def body(at, edge_first):
        lanes = slice(edge_first, edge_first + LANES)
        for rows, cols in zip(FRAME_ROWS, NODE_COLS):
            totals = [None] * len(rows)
            for col in cols:
                value = picked[col, pl.ds(at, 32), lanes]
                for n, row in enumerate(rows):
                    term = rot[col, row : row + 1, lanes] * value
                    totals[n] = term if totals[n] is None else totals[n] + term
            for row, total in zip(rows, totals):
                emit(row, at, edge_first, total)

    for_chunks(channels, edges, 32, body)


def cot_kernel(target, counts, cot, wigner, b0, b1, b2, rot, picked):
    atoms, channels = cot.shape[1:]
    edges = target.shape[1]
    rot[...] = wigner[...].astype(F32)
    bmat = (b0, b1, b2)
    live = lax.broadcasted_iota(jnp.int32, (1, edges), 1) < counts[0, 0]
    gather((cot,), one_hot(atoms, jnp.where(live, target[...], -1)), picked)

    def emit(row, at, edge_first, total):
        which, block, half = place(row)
        rows = pl.ds(pl.multiple_of(block * channels + at, 32), 32)
        lanes = slice(half * edges + edge_first, half * edges + edge_first + LANES)
        bmat[which][rows, lanes] = total.astype(BF16)

    rotate(rot, picked, emit)


def grad_kernel(
    source, feats_core, feats_own, feats_far, wigner, radial, b0, b1, b2,
    keep_a, keep_b, send_a, send_b,
    rot, gate, picked, a0, a1, a2, grad,
):
    atoms, channels = feats_own.shape[1:]
    edges = source.shape[1]
    rot[...] = wigner[...].astype(F32)
    gate[...] = radial[...].astype(F32).T
    amat = (a0, a1, a2)
    gather((feats_core, feats_own, feats_far), near_pick(source, atoms), picked)

    def emit(row, at, edge_first, total):
        which, block, half = place(row)
        rows = pl.ds(pl.multiple_of(block * channels + at, 32), 32)
        gated = total * gate[pl.ds(at, 32), edge_first : edge_first + LANES]
        lanes = slice(half * edges + edge_first, half * edges + edge_first + LANES)
        amat[which][rows, lanes] = gated.astype(BF16)

    rotate(rot, picked, emit)

    def put(first, blocks, block, product):
        for n in range(product.shape[1] // LANES):
            grad[pl.ds(first + block + n, blocks * LANES, stride=blocks), :] = product[
                :, n * LANES : (n + 1) * LANES
            ]

    firsts = first_rows()
    for order, (left, right) in enumerate(((a0, b0), (a1, b1), (a2, b2))):
        blocks = 5 - order
        first = firsts[max(2 * order - 1, 0)]
        for block in range(0, blocks, 2):
            width = min(2, blocks - block)
            part = right[block * LANES : (block + width) * LANES, :]
            put(first, blocks, block, nt(left[...], part))
            if order:
                product = nt(left[:, :edges], part[:, edges:]) - nt(left[:, edges:], part[:, :edges])
                put(firsts[2 * order], blocks, block, product)
    shards, rows_a, rows_b = keep_a.shape[0], keep_a.shape[1], keep_b.shape[1]
    rows = rows_a + rows_b
    parity = lax.rem(lax.axis_index("graph"), 2)
    for n in range(shards):
        at = (2 * n + 1 - parity) * rows
        send_a[n] = grad[pl.ds(at, rows_a), :].astype(BF16)
        send_b[n] = grad[pl.ds(at + rows_a, rows_b), :].astype(BF16)
        at = (2 * n + parity) * rows
        keep_a[n] = grad[pl.ds(at, rows_a), :]
        keep_b[n] = grad[pl.ds(at + rows_a, rows_b), :]


def backward_kernel(
    source, near, far, b0, b1, b2, wigner, radial,
    out_core, out_own, out_far,
    rot, gate, flat, w0, w1r, w1i, w2r, w2i, back, spread,
):
    coefs, atoms, channels = out_own.shape
    edges = source.shape[1]
    rot[...] = wigner[...].astype(F32)
    gate[...] = radial[...].astype(F32).T
    index = lax.axis_index("graph")
    pieces_each, rows = near.shape[:2]
    order = gather_order(pieces_each.bit_length())[:-1]
    for first, pieces in ((0, near), (1, far)):
        for n in range(pieces_each):
            offset = sum(((n >> j) & 1) << order[j] for j in range(len(order)))
            shard = index ^ (offset + first)
            flat[pl.ds(shard * rows, rows), :] = pieces[n].astype(F32)
    for matrix, blocks, first in zip((w0, w1r, w1i, w2r, w2i), WEIGHTS, first_rows()):
        for block in range(blocks):
            matrix[:, block * LANES : (block + 1) * LANES] = flat[
                pl.ds(first + block, blocks * LANES, stride=blocks), :
            ].astype(BF16)

    dot = functools.partial(jnp.dot, preferred_element_type=F32)
    for row in range(5):
        rows = slice(row * channels, (row + 1) * channels)
        back[row] = dot(w0[rows, :], b0[...]) * gate[...]
    for first, real, imag, both, blocks in ((5, w1r, w1i, b1, 4), (13, w2r, w2i, b2, 3)):
        for block in range(blocks):
            rows = slice(block * channels, (block + 1) * channels)
            straight = dot(real[rows, :], both[...])
            crossed = dot(imag[rows, :], both[...])
            back[first + block] = (straight[:, :edges] + crossed[:, edges:]) * gate[...]
            back[first + blocks + block] = (straight[:, edges:] - crossed[:, :edges]) * gate[...]

    def body(at, edge_first):
        lanes = slice(edge_first, edge_first + LANES)
        for rows, cols in zip(FRAME_ROWS, NODE_COLS):
            totals = [None] * len(cols)
            for row in rows:
                value = back[row, pl.ds(at, 16), lanes]
                for n, col in enumerate(cols):
                    term = rot[col, row : row + 1, lanes] * value
                    totals[n] = term if totals[n] is None else totals[n] + term
            for col, total in zip(cols, totals):
                spread[col, pl.ds(at, 16), lanes] = total.astype(BF16)

    for_chunks(channels, edges, 16, body)
    pick = near_pick(source, atoms)
    for col in range(coefs):
        block = nt(pick, spread[col])
        out_core[col] = block[:atoms].astype(BF16)
        out_own[col] = block[atoms : 2 * atoms]
        out_far[col] = block[2 * atoms :].astype(BF16)


def expert_kernel(mixing, own_rows, *refs):
    systems, experts_all = mixing.shape
    others, out, wide = refs[: systems - 1], refs[systems - 1], refs[systems]
    experts, columns = out.shape
    rows = columns // LANES
    position = lax.axis_index("dp")

    @pl.when(pl.program_id(0) == 0)
    def _():
        for n, other in enumerate(others):
            wide[n] = other[...].astype(F32)

    spot = lax.broadcasted_iota(jnp.int32, (experts, experts_all), 1)
    mine = lax.broadcasted_iota(jnp.int32, (experts, experts_all), 0) + position * experts
    scales = []
    for n in range(systems):
        system = lax.rem(position - n + systems, systems)
        row = mixing[pl.ds(system, 1), :]
        column = jnp.sum(jnp.where(spot == mine, row, 0.0), axis=1, keepdims=True)
        scales.append(jnp.broadcast_to(column, (experts, LANES)))
    base = pl.program_id(0) * rows
    group = 12

    def step(turn, unused):
        for n in range(group):
            at = turn * group + n
            total = own_rows[pl.ds(base + at, 1), :] * scales[0]
            for other in range(systems - 1):
                total = total + wide[other, pl.ds(base + at, 1), :] * scales[other + 1]
            out[:, pl.ds(pl.multiple_of(at * LANES, LANES), LANES)] = total
        return unused

    lax.fori_loop(0, rows // group, step, 0)


def spec(space=pltpu.VMEM):
    return pl.BlockSpec(memory_space=space)


KCOST = 1000
PARAMS = pltpu.CompilerParams(vmem_limit_bytes=56 * 1024 * 1024)


def cost(flops, size):
    return pl.CostEstimate(flops=flops, bytes_accessed=size, transcendentals=0)


def gather_order(bits):
    return list(reversed(range(bits)))


def swap(x, bit):
    size = lax.axis_size("graph")
    return lax.ppermute(x, "graph", [(i, i ^ (1 << bit)) for i in range(size)])


def across(x):
    size = lax.axis_size("graph")
    pairs = [(i, i + 1) for i in range(1, size - 1, 2)]
    return lax.ppermute(x, "graph", pairs + [(j, i) for i, j in pairs])


def after(x, *others):
    return lax.optimization_barrier((x,) + others)[0]


def on_device(
    node_feats, node_cot, wigner, radial, source_atom, target_index, edge_counts,
    merged_weights, mixing,
):
    atoms, coefs, channels = node_feats.shape[1:]
    edges = source_atom.shape[1]
    size = lax.axis_size("graph")
    bits = size.bit_length() - 1
    index = lax.axis_index("graph")
    shard_rows = merged_weights.shape[1] // LANES
    total_rows = shard_rows * size
    half = size // 2
    rows_a = (shard_rows // 2 + 7) // 8 * 8
    split = (rows_a, shard_rows - rows_a)

    weight_bits = gather_order(bits)
    held = merged_weights.reshape(1, shard_rows, LANES)
    came = swap(held, weight_bits[0])

    feats = jnp.transpose(node_feats[0], (1, 0, 2))
    feats_far = across(feats)
    feats_core = swap(feats, 0)
    rotation = jnp.transpose(wigner[0], (1, 0, 2))

    shapes = [(5, 1), (4, 2), (3, 2)]
    rot_scratch = pltpu.VMEM((coefs, 19, edges), F32)
    gate_scratch = pltpu.VMEM((channels, edges), F32)
    picked_scratch = pltpu.VMEM((coefs, channels, edges), F32)
    bmats = pl.pallas_call(
        cot_kernel,
        out_shape=[
            jax.ShapeDtypeStruct((g * channels, h * edges), BF16) for g, h in shapes
        ],
        in_specs=[spec(), spec(pltpu.SMEM), spec(), spec()],
        out_specs=[spec()] * 3,
        scratch_shapes=[rot_scratch, picked_scratch],
        compiler_params=PARAMS,
        cost_estimate=cost(KCOST, KCOST),
        name="cotangents",
    )(target_index, edge_counts, jnp.transpose(node_cot[0], (1, 0, 2)), rotation)
    came = after(came, bmats[0])
    held = jnp.concatenate([held, came], axis=0)
    came, held, feats_far = lax.optimization_barrier((came, held, feats_far))
    came = swap(held, weight_bits[1])

    keeps_sends = pl.pallas_call(
        grad_kernel,
        out_shape=[
            jax.ShapeDtypeStruct((half, rows, LANES), kind)
            for kind in (F32, BF16)
            for rows in split
        ],
        in_specs=[spec()] * 9,
        out_specs=[spec()] * 4,
        scratch_shapes=[
            rot_scratch,
            gate_scratch,
            picked_scratch,
            pltpu.VMEM((5 * channels, edges), BF16),
            pltpu.VMEM((4 * channels, 2 * edges), BF16),
            pltpu.VMEM((3 * channels, 2 * edges), BF16),
            pltpu.VMEM((total_rows, LANES), F32),
        ],
        compiler_params=PARAMS,
        cost_estimate=cost(KCOST, KCOST),
        name="gradients",
    )(source_atom, feats_core, feats, feats_far, rotation, radial[0], *bmats)
    keeps, sends = keeps_sends[:2], keeps_sends[2:]
    *sends, came = lax.optimization_barrier((*sends, came))

    held = jnp.concatenate([held, came], axis=0)
    came = swap(held, weight_bits[2])

    halving = list(range(1, bits))
    halving = halving[1:2] + halving[:1] + halving[2:]
    totals = [
        (keep + swap(send, 0).astype(F32)).reshape((2,) * (bits - 1) + keep.shape[1:])
        for keep, send in zip(keeps, sends)
    ]
    left = list(reversed(range(1, bits)))
    for turn, bit in enumerate(halving):
        axis = left.index(bit)
        left.remove(bit)
        side = (index >> bit) & 1
        moved = []
        for total in totals:
            pick = functools.partial(
                lax.dynamic_index_in_dim, total, axis=axis, keepdims=False
            )
            moved.append((pick(side), pick(1 - side).astype(BF16)))
        if turn > 0 and turn + 2 < len(weight_bits):
            came = after(came, moved[0][1])
            held = jnp.concatenate([held, came], axis=0)
            came = swap(held, weight_bits[turn + 2])
        totals = [stay + swap(away, bit).astype(F32) for stay, away in moved]
    came = after(came, moved[1][1])
    share = jnp.concatenate(totals, axis=0)

    systems = lax.axis_size("dp")
    rounded = share.astype(BF16)
    others = [
        lax.ppermute(rounded, "dp", [(i, (i + n) % systems) for i in range(systems)])
        for n in range(1, systems)
    ]
    own_experts = mixing.shape[1] // systems
    blocks = 5
    expert_part = pl.pallas_call(
        expert_kernel,
        grid=(blocks,),
        out_shape=jax.ShapeDtypeStruct((own_experts, shard_rows * LANES), F32),
        in_specs=[spec()] * (1 + systems),
        out_specs=pl.BlockSpec((own_experts, shard_rows * LANES // blocks), lambda i: (0, i)),
        scratch_shapes=[pltpu.VMEM((max(systems - 1, 1), shard_rows, LANES), F32)],
        compiler_params=PARAMS,
        cost_estimate=cost(KCOST, KCOST),
        name="experts",
    )(mixing, share, *others)

    grads_core, grads_own, grads_far = pl.pallas_call(
        backward_kernel,
        out_shape=[
            jax.ShapeDtypeStruct((coefs, atoms, channels), kind) for kind in (BF16, F32, BF16)
        ],
        in_specs=[spec()] * 8,
        out_specs=[spec()] * 3,
        scratch_shapes=[
            rot_scratch,
            gate_scratch,
            pltpu.VMEM((total_rows, LANES), F32),
        ]
        + [pltpu.VMEM((g * channels, g * channels), BF16) for g in WEIGHTS]
        + [
            pltpu.VMEM((19, channels, edges), F32),
            pltpu.VMEM((coefs, channels, edges), BF16),
        ],
        compiler_params=PARAMS,
        cost_estimate=cost(KCOST, KCOST),
        name="backward",
    )(source_atom, held, came, *bmats, rotation, radial[0])
    total = grads_own + swap(grads_core, 0).astype(F32) + across(grads_far).astype(F32)
    atom_grads = jnp.transpose(total, (1, 0, 2))[None]
    return (atom_grads, expert_part)


def solution(mesh):
    in_specs = (
        P("dp", "graph", None, None),
        P("dp", "graph", None, None),
        P("dp", None, None, "graph"),
        P("dp", "graph", None),
        P("dp", "graph"),
        P("dp", "graph"),
        P("dp", "graph"),
        P("dp", "graph"),
        P(),
    )
    out_specs = (P("dp", "graph", None, None), P("dp", "graph"))
    return jax.shard_map(
        on_device, mesh=mesh, in_specs=in_specs, out_specs=out_specs, check_vma=False
    )
```

```python
import functools
import itertools

import jax
import jax.numpy as jnp
from jax import lax
from jax.experimental import pallas as pl
from jax.experimental.pallas import tpu as pltpu
from jax.sharding import PartitionSpec as P

BF16 = jnp.bfloat16
F32 = jnp.float32
LANES = 128
GROUPS = ((0, 5), (5, 9), (9, 13), (13, 16), (16, 19))
FRAME_ROWS = tuple(
    tuple(
        first + degree - order
        for first, order in ((0, 0), (5, 1), (9, 1), (13, 2), (16, 2))
        if degree >= order
    )
    for degree in range(5)
)
NODE_COLS = tuple(tuple(range(l * l, (l + 1) * (l + 1))) for l in range(5))
WEIGHTS = (5, 4, 4, 3, 3)


def first_rows():
    rows, out = 0, []
    for group_rows in WEIGHTS:
        out.append(rows)
        rows += group_rows * group_rows * LANES
    return out


def place(row):
    if row < 5:
        return 0, row, 0
    if row < 13:
        return 1, (row - 5) % 4, (row - 5) // 4
    return 2, (row - 13) % 3, (row - 13) // 3


def for_chunks(channels, edges, size, body):
    for edge_first in range(0, edges, LANES):

        def step(turn, unused, edge_first=edge_first):
            body(pl.multiple_of(turn * size, size), edge_first)
            return unused

        lax.fori_loop(0, channels // size, step, 0)


def nt(left, right):
    return lax.dot_general(left, right, (((1,), (1,)), ((), ())), preferred_element_type=F32)


def tn(left, right):
    return lax.dot_general(left, right, (((0,), (0,)), ((), ())), preferred_element_type=F32)


def one_hot(count, wanted):
    edges = wanted.shape[1]
    hit = lax.broadcasted_iota(jnp.int32, (count, edges), 0) == wanted
    return hit.astype(F32).astype(BF16)


def near_pick(source, atoms):
    index = lax.axis_index("graph")
    shard = lax.div(source[...], atoms)
    slot = jnp.where(shard == index, 1, jnp.where(shard == (index ^ 1), 0, 2))
    return one_hot(3 * atoms, (slot - shard) * atoms + source[...])


def gather(pieces, pick, picked):
    for coef in range(picked.shape[0]):
        parts = [piece[coef].astype(F32) for piece in pieces]
        block = parts[0] if len(parts) == 1 else jnp.concatenate(parts, axis=0)
        picked[coef] = tn(block.astype(BF16), pick)


def rotate(rot, picked, emit):
    channels, edges = picked.shape[1:]

    def body(at, edge_first):
        lanes = slice(edge_first, edge_first + LANES)
        for rows, cols in zip(FRAME_ROWS, NODE_COLS):
            totals = [None] * len(rows)
            for col in cols:
                value = picked[col, pl.ds(at, 32), lanes]
                for n, row in enumerate(rows):
                    term = rot[col, row : row + 1, lanes] * value
                    totals[n] = term if totals[n] is None else totals[n] + term
            for row, total in zip(rows, totals):
                emit(row, at, edge_first, total)

    for_chunks(channels, edges, 32, body)


def cot_kernel(
    source, target, counts, cot, feats, wigner, radial,
    b0, b1, b2, rot, gate, pick, feats_near,
    source_v, target_v, cot_v, wigner_v, radial_v, sems, picked,
):
    pairs = (
        (target, target_v), (cot, cot_v), (wigner, wigner_v), (radial, radial_v),
        (source, source_v), (feats, feats_near),
    )
    copies = [pltpu.make_async_copy(*pair, sems.at[n]) for n, pair in enumerate(pairs)]
    for copy in copies:
        copy.start()
    atoms, channels = cot.shape[1:]
    edges = target.shape[1]
    copies[0].wait()
    copies[1].wait()
    bmat = (b0, b1, b2)
    live = lax.broadcasted_iota(jnp.int32, (1, edges), 1) < counts[0, 0]
    gather((cot_v,), one_hot(atoms, jnp.where(live, target_v[...], -1)), picked)
    copies[2].wait()
    rot[...] = wigner_v[...].astype(F32)

    def emit(row, at, edge_first, total):
        which, block, half = place(row)
        rows = pl.ds(pl.multiple_of(block * channels + at, 32), 32)
        lanes = slice(half * edges + edge_first, half * edges + edge_first + LANES)
        bmat[which][rows, lanes] = total.astype(BF16)

    rotate(rot, picked, emit)
    for copy in copies[3:]:
        copy.wait()
    gate[...] = radial_v[...].astype(F32).T
    pick[...] = near_pick(source_v, atoms)


def grad_kernel(
    feats_core, feats_own, feats_far, rot, gate, pick, b0, b1, b2,
    keep_a, keep_b, send_a, send_b,
    picked, a0, a1, a2, grad,
):
    channels, edges = gate.shape
    amat = (a0, a1, a2)
    gather((feats_core, feats_own, feats_far), pick[...], picked)

    def emit(row, at, edge_first, total):
        which, block, half = place(row)
        rows = pl.ds(pl.multiple_of(block * channels + at, 32), 32)
        gated = total * gate[pl.ds(at, 32), edge_first : edge_first + LANES]
        lanes = slice(half * edges + edge_first, half * edges + edge_first + LANES)
        amat[which][rows, lanes] = gated.astype(BF16)

    rotate(rot, picked, emit)

    def put(first, blocks, block, product):
        for n in range(product.shape[1] // LANES):
            grad[pl.ds(first + block + n, blocks * LANES, stride=blocks), :] = product[
                :, n * LANES : (n + 1) * LANES
            ]

    firsts = first_rows()
    for order, (left, right) in enumerate(((a0, b0), (a1, b1), (a2, b2))):
        blocks = 5 - order
        first = firsts[max(2 * order - 1, 0)]
        for block in range(0, blocks, 2):
            width = min(2, blocks - block)
            part = right[block * LANES : (block + width) * LANES, :]
            put(first, blocks, block, nt(left[...], part))
            if order:
                product = nt(left[:, :edges], part[:, edges:]) - nt(left[:, edges:], part[:, :edges])
                put(firsts[2 * order], blocks, block, product)
    rows_a, rows_b = keep_a.shape[-2], keep_b.shape[-2]
    rows = rows_a + rows_b
    parity = lax.rem(lax.axis_index("graph"), 2)
    for n, spot in enumerate(spots(keep_a)):
        at = (2 * n + 1 - parity) * rows
        send_a[spot] = grad[pl.ds(at, rows_a), :].astype(BF16)
        send_b[spot] = grad[pl.ds(at + rows_a, rows_b), :].astype(BF16)
        at = (2 * n + parity) * rows
        keep_a[spot] = grad[pl.ds(at, rows_a), :]
        keep_b[spot] = grad[pl.ds(at + rows_a, rows_b), :]


def spots(ref):
    return itertools.product(*(range(n) for n in ref.shape[:-2]))


def halve_kernel(axis, bit, keep, came, stay, away):
    side = (lax.axis_index("graph") >> bit) & 1
    for spot in spots(stay):
        here = (*spot[:axis], side, *spot[axis:])
        there = (*spot[:axis], 1 - side, *spot[axis:])
        at = spot or Ellipsis
        stay[at] = keep[here] + came[here].astype(F32)
        away[at] = (keep[there] + came[there].astype(F32)).astype(BF16)


def finish_kernel(keep, came, share, rounded):
    total = keep[...] + came[...].astype(F32)
    share[...] = total
    rounded[...] = total.astype(BF16)


def backward_kernel(masks, high, *refs):
    pieces, refs = refs[: len(masks)], refs[len(masks) :]
    b0, b1, b2, rot, gate, pick, out_core, out_own, out_far = refs[:9]
    flat, w0, w1r, w1i, w2r, w2i, back, spread = refs[9:]
    coefs, atoms, channels = out_own.shape
    edges = gate.shape[1]
    index = lax.axis_index("graph")
    rows = pieces[0].shape[1]
    for mask, piece in zip(masks, pieces):
        for n in range(2):
            shard = index ^ (mask + n * high)
            flat[pl.ds(shard * rows, rows), :] = piece[n].astype(F32)
    for matrix, blocks, first in zip((w0, w1r, w1i, w2r, w2i), WEIGHTS, first_rows()):
        for block in range(blocks):
            matrix[:, block * LANES : (block + 1) * LANES] = flat[
                pl.ds(first + block, blocks * LANES, stride=blocks), :
            ].astype(BF16)

    dot = functools.partial(jnp.dot, preferred_element_type=F32)
    for row in range(5):
        rows = slice(row * channels, (row + 1) * channels)
        back[row] = dot(w0[rows, :], b0[...]) * gate[...]
    for first, real, imag, both, blocks in ((5, w1r, w1i, b1, 4), (13, w2r, w2i, b2, 3)):
        for block in range(blocks):
            rows = slice(block * channels, (block + 1) * channels)
            straight = dot(real[rows, :], both[...])
            crossed = dot(imag[rows, :], both[...])
            back[first + block] = (straight[:, :edges] + crossed[:, edges:]) * gate[...]
            back[first + blocks + block] = (straight[:, edges:] - crossed[:, :edges]) * gate[...]

    def body(at, edge_first):
        lanes = slice(edge_first, edge_first + LANES)
        for rows, cols in zip(FRAME_ROWS, NODE_COLS):
            totals = [None] * len(cols)
            for row in rows:
                value = back[row, pl.ds(at, 16), lanes]
                for n, col in enumerate(cols):
                    term = rot[col, row : row + 1, lanes] * value
                    totals[n] = term if totals[n] is None else totals[n] + term
            for col, total in zip(cols, totals):
                spread[col, pl.ds(at, 16), lanes] = total.astype(BF16)

    for_chunks(channels, edges, 16, body)
    for col in range(coefs):
        block = nt(pick[...], spread[col])
        out_core[col] = block[:atoms].astype(BF16)
        out_own[col] = block[atoms : 2 * atoms]
        out_far[col] = block[2 * atoms :].astype(BF16)


def expert_kernel(first_row, mixing, own_rows, *refs):
    systems, experts_all = mixing.shape
    others, (out, wide, block, sems) = refs[: systems - 1], refs[-4:]
    experts = out.shape[0]
    rows = own_rows.shape[0]
    position = lax.axis_index("dp")
    for n, other in enumerate(others):
        wide[n] = other[...].astype(F32)
    spot = lax.broadcasted_iota(jnp.int32, (experts, experts_all), 1)
    mine = lax.broadcasted_iota(jnp.int32, (experts, experts_all), 0) + position * experts
    scales = []
    for n in range(systems):
        system = lax.rem(position - n + systems, systems)
        row = mixing[pl.ds(system, 1), :]
        column = jnp.sum(jnp.where(spot == mine, row, 0.0), axis=1, keepdims=True)
        scales.append(jnp.broadcast_to(column, (experts, LANES)))
    chunk = rows // 2
    group = max(g for g in range(1, 9) if chunk % g == 0)
    copies = []
    for part in range(2):

        def step(turn, unused, part=part):
            for n in range(group):
                at = part * chunk + turn * group + n
                total = own_rows[pl.ds(at, 1), :] * scales[0]
                for other in range(systems - 1):
                    total = total + wide[other, pl.ds(at, 1), :] * scales[other + 1]
                block[:, pl.ds(pl.multiple_of(at * LANES, LANES), LANES)] = total
            return unused

        lax.fori_loop(0, chunk // group, step, 0)
        here = slice(part * chunk * LANES, (part + 1) * chunk * LANES)
        there = slice(here.start + first_row * LANES, here.stop + first_row * LANES)
        copy = pltpu.make_async_copy(block.at[:, here], out.at[:, there], sems.at[part])
        copy.start()
        copies.append(copy)
    for copy in copies:
        copy.wait()


def spec(space=pltpu.VMEM):
    return pl.BlockSpec(memory_space=space)


KCOST = 1000


def limit(mebibytes):
    return pltpu.CompilerParams(vmem_limit_bytes=mebibytes * 1024 * 1024)


def cost(flops, size):
    return pl.CostEstimate(flops=flops, bytes_accessed=size, transcendentals=0)


def swap(x, bit):
    size = lax.axis_size("graph")
    return lax.ppermute(x, "graph", [(i, i ^ (1 << bit)) for i in range(size)])


def across(x):
    size = lax.axis_size("graph")
    pairs = [(i, i + 1) for i in range(1, size - 1, 2)]
    return lax.ppermute(x, "graph", pairs + [(j, i) for i, j in pairs])


def in_hbm(x):
    return pltpu.with_memory_space_constraint(x, pltpu.HBM)


def after(x, *others):
    return lax.optimization_barrier((x,) + others)[0]


def on_device(
    node_feats, node_cot, wigner, radial, source_atom, target_index, edge_counts,
    merged_weights, mixing,
):
    atoms, coefs, channels = node_feats.shape[1:]
    edges = source_atom.shape[1]
    size = lax.axis_size("graph")
    bits = size.bit_length() - 1
    shard_rows = merged_weights.shape[1] // LANES
    total_rows = shard_rows * size
    rows_a = (shard_rows // 2 + 7) // 8 * 8
    split = (rows_a, shard_rows - rows_a)

    feats = jnp.transpose(node_feats[0], (1, 0, 2))
    feats_far = across(feats)
    feats_core = swap(feats, 0)
    target, feats_core = lax.optimization_barrier((target_index, feats_core))

    held = merged_weights.reshape(1, shard_rows, LANES)
    came = swap(held, bits - 1)

    hbm = spec(pltpu.HBM)
    picked_scratch = pltpu.VMEM((coefs, channels, edges), F32)
    *bmats, rot, gate, pick, feats_near = pl.pallas_call(
        cot_kernel,
        out_shape=[
            pltpu.VMEM((5 * channels, edges), BF16),
            pltpu.VMEM((4 * channels, 2 * edges), BF16),
            pltpu.VMEM((3 * channels, 2 * edges), BF16),
            pltpu.VMEM((coefs, 19, edges), F32),
            pltpu.VMEM((channels, edges), F32),
            jax.ShapeDtypeStruct((3 * atoms, edges), BF16),
            pltpu.VMEM((coefs, atoms, channels), BF16),
        ],
        in_specs=[hbm, hbm, spec(pltpu.SMEM), hbm, hbm, hbm, hbm],
        out_specs=[spec()] * 7,
        scratch_shapes=[
            pltpu.VMEM((1, edges), jnp.int32),
            pltpu.VMEM((1, edges), jnp.int32),
            pltpu.VMEM((coefs, atoms, channels), BF16),
            pltpu.VMEM((coefs, 19, edges), BF16),
            pltpu.VMEM((edges, channels), BF16),
            pltpu.SemaphoreType.DMA((6,)),
            picked_scratch,
        ],
        compiler_params=limit(12),
        cost_estimate=cost(KCOST, KCOST),
        name="cotangents",
    )(
        in_hbm(source_atom), in_hbm(target), edge_counts,
        in_hbm(jnp.transpose(node_cot[0], (1, 0, 2))), in_hbm(feats),
        in_hbm(jnp.transpose(wigner[0], (1, 0, 2))), in_hbm(radial[0]),
    )

    came = after(came, pick)
    held = jnp.concatenate([held, came], axis=0)
    held, feats_far = lax.optimization_barrier((held, feats_far))
    near, up = bits - 2, bits - 3
    pieces = {0: held, 1 << near: swap(held, near), 1 << up: swap(held, up)}

    keeps_sends = pl.pallas_call(
        grad_kernel,
        out_shape=[
            kind((2,) * (bits - 1) + (rows, LANES), dtype)
            for kind, dtype in ((pltpu.VMEM, F32), (jax.ShapeDtypeStruct, BF16))
            for rows in split
        ],
        in_specs=[spec()] * 9,
        out_specs=[spec()] * 4,
        scratch_shapes=[
            picked_scratch,
            pltpu.VMEM((5 * channels, edges), BF16),
            pltpu.VMEM((4 * channels, 2 * edges), BF16),
            pltpu.VMEM((3 * channels, 2 * edges), BF16),
            pltpu.VMEM((total_rows, LANES), F32),
        ],
        compiler_params=limit(17),
        cost_estimate=cost(KCOST, KCOST),
        name="gradients",
    )(feats_core, feats_near, feats_far, rot, gate, pick, *bmats)
    keeps, sends = keeps_sends[:2], list(keeps_sends[2:])
    *sends, pieces[1 << near], pieces[1 << up] = lax.optimization_barrier(
        (*sends, pieces[1 << near], pieces[1 << up])
    )
    pieces[1 << near | 1 << up] = swap(pieces[1 << near], up)

    low_to_high = list(range(1, bits))
    orders = [low_to_high, low_to_high[1:] + low_to_high[:1]]
    left = [list(reversed(low_to_high)) for _ in orders]

    def halve(turn, keeps, cames):
        stays, aways = [], []
        for part, (keep, came) in enumerate(zip(keeps, cames)):
            bit = orders[part][turn]
            axis = left[part].index(bit)
            left[part].remove(bit)
            shape = (2,) * len(left[part]) + came.shape[-2:]
            stay, away = pl.pallas_call(
                functools.partial(halve_kernel, axis, bit),
                out_shape=[pltpu.VMEM(shape, F32), jax.ShapeDtypeStruct(shape, BF16)],
                in_specs=[spec()] * 2,
                out_specs=[spec()] * 2,
                compiler_params=limit(6),
                cost_estimate=cost(KCOST, KCOST),
                name="halve",
            )(keep, came)
            stays.append(stay)
            aways.append(away)
        return stays, aways

    def exchange(turn, aways):
        return [swap(away, orders[part][turn]) for part, away in enumerate(aways)]

    stays, aways = halve(0, keeps, [swap(send, 0) for send in sends])

    def fan_out(some):
        some = dict(some)
        for bit in reversed(range(up)):
            some.update({mask | 1 << bit: swap(some[mask], bit) for mask in list(some)})
        return some

    last = pieces.pop(1 << near | 1 << up)
    pieces = fan_out(pieces)
    cames = exchange(0, aways)
    for turn in range(1, bits - 1):
        stays, aways = halve(turn, stays, cames)
        masks = list(pieces)
        together = lax.optimization_barrier((*aways, *pieces.values()))
        aways, pieces = together[:2], dict(zip(masks, together[2:]))
        if turn == bits - 2:
            pieces.update(fan_out({1 << near | 1 << up: after(last, *aways)}))
        cames = exchange(turn, aways)
    cames = lax.optimization_barrier(cames)

    systems = lax.axis_size("dp")
    shares, roundeds = [], []
    for stay, came in zip(stays, cames):
        share, rounded = pl.pallas_call(
            finish_kernel,
            out_shape=[pltpu.VMEM(came.shape, F32), jax.ShapeDtypeStruct(came.shape, BF16)],
            in_specs=[spec()] * 2,
            out_specs=[spec()] * 2,
            compiler_params=limit(6),
            cost_estimate=cost(KCOST, KCOST),
            name="finish",
        )(stay, came)
        shares.append(share)
        roundeds.append(rounded)

    masks = list(pieces)
    ready = list(pieces.values())
    grads_core, grads_own, grads_far = pl.pallas_call(
        functools.partial(backward_kernel, masks, 1 << (bits - 1)),
        out_shape=[
            jax.ShapeDtypeStruct((coefs, atoms, channels), kind) for kind in (BF16, F32, BF16)
        ],
        in_specs=[spec()] * (6 + len(masks)),
        out_specs=[spec()] * 3,
        scratch_shapes=[pltpu.VMEM((total_rows, LANES), F32)]
        + [pltpu.VMEM((g * channels, g * channels), BF16) for g in WEIGHTS]
        + [
            pltpu.VMEM((19, channels, edges), F32),
            pltpu.VMEM((coefs, channels, edges), BF16),
        ],
        compiler_params=limit(18),
        cost_estimate=cost(KCOST, KCOST),
        name="backward",
    )(*ready[: len(masks)], *bmats, rot, gate, pick)
    total = grads_own + swap(grads_core, 0).astype(F32) + across(grads_far).astype(F32)
    atom_grads = jnp.transpose(total, (1, 0, 2))[None]

    own_experts = mixing.shape[1] // systems
    expert_part = None
    for first_row, share, rounded in zip((0, rows_a), shares, roundeds):
        others = [
            lax.ppermute(rounded, "dp", [(i, (i + n) % systems) for i in range(systems)])
            for n in range(1, systems)
        ]
        rows = share.shape[0]
        before = [] if expert_part is None else [expert_part]
        expert_part = pl.pallas_call(
            functools.partial(expert_kernel, first_row),
            out_shape=jax.ShapeDtypeStruct((own_experts, shard_rows * LANES), F32),
            in_specs=[spec()] * (1 + systems) + [spec(pl.ANY)] * len(before),
            out_specs=spec(pl.ANY),
            input_output_aliases={1 + systems: 0} if before else {},
            scratch_shapes=[
                pltpu.VMEM((max(systems - 1, 1), rows, LANES), F32),
                pltpu.VMEM((own_experts, rows * LANES), F32),
                pltpu.SemaphoreType.DMA((2,)),
            ],
            compiler_params=limit(4),
            cost_estimate=cost(KCOST, KCOST),
            name="experts",
        )(mixing, share, *others, *before)
    return (atom_grads, expert_part)


def solution(mesh):
    in_specs = (
        P("dp", "graph", None, None),
        P("dp", "graph", None, None),
        P("dp", None, None, "graph"),
        P("dp", "graph", None),
        P("dp", "graph"),
        P("dp", "graph"),
        P("dp", "graph"),
        P("dp", "graph"),
        P(),
    )
    out_specs = (P("dp", "graph", None, None), P("dp", "graph"))
    return jax.shard_map(
        on_device, mesh=mesh, in_specs=in_specs, out_specs=out_specs, check_vma=False
    )
```

```python
import functools
import itertools

import jax
import jax.numpy as jnp
from jax import lax
from jax.experimental import pallas as pl
from jax.experimental.pallas import tpu as pltpu
from jax.sharding import PartitionSpec as P

BF16 = jnp.bfloat16
F32 = jnp.float32
LANES = 128
GROUPS = ((0, 5), (5, 9), (9, 13), (13, 16), (16, 19))
FRAME_ROWS = tuple(
    tuple(
        first + degree - order
        for first, order in ((0, 0), (5, 1), (9, 1), (13, 2), (16, 2))
        if degree >= order
    )
    for degree in range(5)
)
NODE_COLS = tuple(tuple(range(l * l, (l + 1) * (l + 1))) for l in range(5))
WEIGHTS = (5, 4, 4, 3, 3)


def first_rows():
    rows, out = 0, []
    for group_rows in WEIGHTS:
        out.append(rows)
        rows += group_rows * group_rows * LANES
    return out


def place(row):
    if row < 5:
        return 0, row, 0
    if row < 13:
        return 1, (row - 5) % 4, (row - 5) // 4
    return 2, (row - 13) % 3, (row - 13) // 3


def for_chunks(channels, edges, size, body):
    for edge_first in range(0, edges, LANES):

        def step(turn, unused, edge_first=edge_first):
            body(pl.multiple_of(turn * size, size), edge_first)
            return unused

        lax.fori_loop(0, channels // size, step, 0)


def nt(left, right):
    return lax.dot_general(left, right, (((1,), (1,)), ((), ())), preferred_element_type=F32)


def tn(left, right):
    return lax.dot_general(left, right, (((0,), (0,)), ((), ())), preferred_element_type=F32)


def one_hot(count, wanted):
    edges = wanted.shape[1]
    hit = lax.broadcasted_iota(jnp.int32, (count, edges), 0) == wanted
    return hit.astype(F32).astype(BF16)


def near_pick(source, atoms):
    index = lax.axis_index("graph")
    shard = lax.div(source[...], atoms)
    slot = jnp.where(shard == index, 1, jnp.where(shard == (index ^ 1), 0, 2))
    return one_hot(3 * atoms, (slot - shard) * atoms + source[...])


def gather(pieces, pick, picked):
    for coef in range(picked.shape[0]):
        parts = [piece[coef].astype(F32) for piece in pieces]
        block = parts[0] if len(parts) == 1 else jnp.concatenate(parts, axis=0)
        picked[coef] = tn(block.astype(BF16), pick)


def rotate(rot, picked, emit):
    channels, edges = picked.shape[1:]

    def body(at, edge_first):
        lanes = slice(edge_first, edge_first + LANES)
        for rows, cols in zip(FRAME_ROWS, NODE_COLS):
            totals = [None] * len(rows)
            for col in cols:
                value = picked[col, pl.ds(at, 32), lanes]
                for n, row in enumerate(rows):
                    term = rot[col, row : row + 1, lanes] * value
                    totals[n] = term if totals[n] is None else totals[n] + term
            for row, total in zip(rows, totals):
                emit(row, at, edge_first, total)

    for_chunks(channels, edges, 32, body)


def cot_kernel(
    source, target, counts, cot, feats, wigner, radial,
    b0, b1, b2, rot, gate, pick, feats_near,
    source_v, target_v, cot_v, wigner_v, radial_v, sems, picked,
):
    pairs = (
        (target, target_v), (cot, cot_v), (wigner, wigner_v), (radial, radial_v),
        (source, source_v), (feats, feats_near),
    )
    copies = [pltpu.make_async_copy(*pair, sems.at[n]) for n, pair in enumerate(pairs)]
    for copy in copies:
        copy.start()
    atoms, channels = cot.shape[1:]
    edges = target.shape[1]
    copies[0].wait()
    copies[1].wait()
    bmat = (b0, b1, b2)
    live = lax.broadcasted_iota(jnp.int32, (1, edges), 1) < counts[0, 0]
    gather((cot_v,), one_hot(atoms, jnp.where(live, target_v[...], -1)), picked)
    copies[2].wait()
    rot[...] = wigner_v[...].astype(F32)

    def emit(row, at, edge_first, total):
        which, block, half = place(row)
        rows = pl.ds(pl.multiple_of(block * channels + at, 32), 32)
        lanes = slice(half * edges + edge_first, half * edges + edge_first + LANES)
        bmat[which][rows, lanes] = total.astype(BF16)

    rotate(rot, picked, emit)
    for copy in copies[3:]:
        copy.wait()
    gate[...] = radial_v[...].astype(F32).T
    pick[...] = near_pick(source_v, atoms)


def grad_kernel(
    feats_core, feats_own, feats_far, rot, gate, pick, b0, b1, b2,
    keep_a, keep_b, send_a, send_b,
    picked, a0, a1, a2, grad,
):
    channels, edges = gate.shape
    amat = (a0, a1, a2)
    gather((feats_core, feats_own, feats_far), pick[...], picked)

    def emit(row, at, edge_first, total):
        which, block, half = place(row)
        rows = pl.ds(pl.multiple_of(block * channels + at, 32), 32)
        gated = total * gate[pl.ds(at, 32), edge_first : edge_first + LANES]
        lanes = slice(half * edges + edge_first, half * edges + edge_first + LANES)
        amat[which][rows, lanes] = gated.astype(BF16)

    rotate(rot, picked, emit)

    def put(first, blocks, block, product):
        for n in range(product.shape[1] // LANES):
            grad[pl.ds(first + block + n, blocks * LANES, stride=blocks), :] = product[
                :, n * LANES : (n + 1) * LANES
            ]

    firsts = first_rows()
    for order, (left, right) in enumerate(((a0, b0), (a1, b1), (a2, b2))):
        blocks = 5 - order
        first = firsts[max(2 * order - 1, 0)]
        for block in range(0, blocks, 2):
            width = min(2, blocks - block)
            part = right[block * LANES : (block + width) * LANES, :]
            put(first, blocks, block, nt(left[...], part))
            if order:
                product = nt(left[:, :edges], part[:, edges:]) - nt(left[:, edges:], part[:, :edges])
                put(firsts[2 * order], blocks, block, product)
    rows_a, rows_b = keep_a.shape[-2], keep_b.shape[-2]
    rows = rows_a + rows_b
    parity = lax.rem(lax.axis_index("graph"), 2)
    for n, spot in enumerate(spots(keep_a)):
        at = (2 * n + 1 - parity) * rows
        send_a[spot] = grad[pl.ds(at, rows_a), :].astype(BF16)
        send_b[spot] = grad[pl.ds(at + rows_a, rows_b), :].astype(BF16)
        at = (2 * n + parity) * rows
        keep_a[spot] = grad[pl.ds(at, rows_a), :]
        keep_b[spot] = grad[pl.ds(at + rows_a, rows_b), :]


def spots(ref):
    return itertools.product(*(range(n) for n in ref.shape[:-2]))


def halve_kernel(axis, bit, keep, came, stay, away):
    side = (lax.axis_index("graph") >> bit) & 1
    for spot in spots(stay):
        here = (*spot[:axis], side, *spot[axis:])
        there = (*spot[:axis], 1 - side, *spot[axis:])
        at = spot or Ellipsis
        stay[at] = keep[here] + came[here].astype(F32)
        away[at] = (keep[there] + came[there].astype(F32)).astype(BF16)


def finish_kernel(keep, came, share, rounded):
    total = keep[...] + came[...].astype(F32)
    share[...] = total
    rounded[...] = total.astype(BF16)


def backward_kernel(masks, high, *refs):
    pieces, refs = refs[: len(masks)], refs[len(masks) :]
    b0, b1, b2, rot, gate, pick, out_core, out_own, out_far = refs[:9]
    flat, w0, w1r, w1i, w2r, w2i, back, spread = refs[9:]
    coefs, atoms, channels = out_own.shape
    edges = gate.shape[1]
    index = lax.axis_index("graph")
    rows = pieces[0].shape[1]
    for mask, piece in zip(masks, pieces):
        for n in range(2):
            shard = index ^ (mask + n * high)
            flat[pl.ds(shard * rows, rows), :] = piece[n].astype(F32)
    for matrix, blocks, first in zip((w0, w1r, w1i, w2r, w2i), WEIGHTS, first_rows()):
        for block in range(blocks):
            matrix[:, block * LANES : (block + 1) * LANES] = flat[
                pl.ds(first + block, blocks * LANES, stride=blocks), :
            ].astype(BF16)

    dot = functools.partial(jnp.dot, preferred_element_type=F32)
    for row in range(5):
        rows = slice(row * channels, (row + 1) * channels)
        back[row] = dot(w0[rows, :], b0[...]) * gate[...]
    for first, real, imag, both, blocks in ((5, w1r, w1i, b1, 4), (13, w2r, w2i, b2, 3)):
        for block in range(blocks):
            rows = slice(block * channels, (block + 1) * channels)
            straight = dot(real[rows, :], both[...])
            crossed = dot(imag[rows, :], both[...])
            back[first + block] = (straight[:, :edges] + crossed[:, edges:]) * gate[...]
            back[first + blocks + block] = (straight[:, edges:] - crossed[:, :edges]) * gate[...]

    def body(at, edge_first):
        lanes = slice(edge_first, edge_first + LANES)
        for rows, cols in zip(FRAME_ROWS, NODE_COLS):
            totals = [None] * len(cols)
            for row in rows:
                value = back[row, pl.ds(at, 16), lanes]
                for n, col in enumerate(cols):
                    term = rot[col, row : row + 1, lanes] * value
                    totals[n] = term if totals[n] is None else totals[n] + term
            for col, total in zip(cols, totals):
                spread[col, pl.ds(at, 16), lanes] = total.astype(BF16)

    for_chunks(channels, edges, 16, body)
    for col in range(coefs):
        block = nt(pick[...], spread[col])
        out_core[col] = block[:atoms].astype(BF16)
        out_own[col] = block[atoms : 2 * atoms]
        out_far[col] = block[2 * atoms :].astype(BF16)


def expert_kernel(first_row, mixing, own_rows, *refs):
    systems, experts_all = mixing.shape
    others, (out, wide, block, sems) = refs[: systems - 1], refs[-4:]
    experts = out.shape[0]
    rows = own_rows.shape[0]
    position = lax.axis_index("dp")
    for n, other in enumerate(others):
        wide[n] = other[...].astype(F32)
    spot = lax.broadcasted_iota(jnp.int32, (experts, experts_all), 1)
    mine = lax.broadcasted_iota(jnp.int32, (experts, experts_all), 0) + position * experts
    scales = []
    for n in range(systems):
        system = lax.rem(position - n + systems, systems)
        row = mixing[pl.ds(system, 1), :]
        column = jnp.sum(jnp.where(spot == mine, row, 0.0), axis=1, keepdims=True)
        scales.append(jnp.broadcast_to(column, (experts, LANES)))
    chunk = rows // 2
    group = max(g for g in range(1, 9) if chunk % g == 0)
    copies = []
    for part in range(2):

        def step(turn, unused, part=part):
            for n in range(group):
                at = part * chunk + turn * group + n
                total = own_rows[pl.ds(at, 1), :] * scales[0]
                for other in range(systems - 1):
                    total = total + wide[other, pl.ds(at, 1), :] * scales[other + 1]
                block[:, pl.ds(pl.multiple_of(at * LANES, LANES), LANES)] = total
            return unused

        lax.fori_loop(0, chunk // group, step, 0)
        here = slice(part * chunk * LANES, (part + 1) * chunk * LANES)
        there = slice(here.start + first_row * LANES, here.stop + first_row * LANES)
        copy = pltpu.make_async_copy(block.at[:, here], out.at[:, there], sems.at[part])
        copy.start()
        copies.append(copy)
    for copy in copies:
        copy.wait()


def spec(space=pltpu.VMEM):
    return pl.BlockSpec(memory_space=space)


KCOST = 1000


def limit(mebibytes):
    return pltpu.CompilerParams(vmem_limit_bytes=mebibytes * 1024 * 1024)


def cost(flops, size):
    return pl.CostEstimate(flops=flops, bytes_accessed=size, transcendentals=0)


def swap(x, bit):
    size = lax.axis_size("graph")
    return lax.ppermute(x, "graph", [(i, i ^ (1 << bit)) for i in range(size)])


def across(x):
    size = lax.axis_size("graph")
    pairs = [(i, i + 1) for i in range(1, size - 1, 2)]
    return lax.ppermute(x, "graph", pairs + [(j, i) for i, j in pairs])


def in_hbm(x):
    return pltpu.with_memory_space_constraint(x, pltpu.HBM)


def after(x, *others):
    return lax.optimization_barrier((x,) + others)[0]


def on_device(
    node_feats, node_cot, wigner, radial, source_atom, target_index, edge_counts,
    merged_weights, mixing,
):
    atoms, coefs, channels = node_feats.shape[1:]
    edges = source_atom.shape[1]
    size = lax.axis_size("graph")
    bits = size.bit_length() - 1
    shard_rows = merged_weights.shape[1] // LANES
    total_rows = shard_rows * size
    rows_a = (shard_rows // 2 + 7) // 8 * 8
    split = (rows_a, shard_rows - rows_a)

    feats = jnp.transpose(node_feats[0], (1, 0, 2))
    feats_far = across(feats)
    feats_core = swap(feats, 0)
    target, feats_core = lax.optimization_barrier((target_index, feats_core))

    held = merged_weights.reshape(1, shard_rows, LANES)
    came = swap(held, bits - 1)

    hbm = spec(pltpu.HBM)
    picked_scratch = pltpu.VMEM((coefs, channels, edges), F32)
    *bmats, rot, gate, pick, feats_near = pl.pallas_call(
        cot_kernel,
        out_shape=[
            pltpu.VMEM((5 * channels, edges), BF16),
            pltpu.VMEM((4 * channels, 2 * edges), BF16),
            pltpu.VMEM((3 * channels, 2 * edges), BF16),
            pltpu.VMEM((coefs, 19, edges), F32),
            pltpu.VMEM((channels, edges), F32),
            jax.ShapeDtypeStruct((3 * atoms, edges), BF16),
            pltpu.VMEM((coefs, atoms, channels), BF16),
        ],
        in_specs=[hbm, hbm, spec(pltpu.SMEM), hbm, hbm, hbm, hbm],
        out_specs=[spec()] * 7,
        scratch_shapes=[
            pltpu.VMEM((1, edges), jnp.int32),
            pltpu.VMEM((1, edges), jnp.int32),
            pltpu.VMEM((coefs, atoms, channels), BF16),
            pltpu.VMEM((coefs, 19, edges), BF16),
            pltpu.VMEM((edges, channels), BF16),
            pltpu.SemaphoreType.DMA((6,)),
            picked_scratch,
        ],
        compiler_params=limit(12),
        cost_estimate=cost(KCOST, KCOST),
        name="cotangents",
    )(
        in_hbm(source_atom), in_hbm(target), edge_counts,
        in_hbm(jnp.transpose(node_cot[0], (1, 0, 2))), in_hbm(feats),
        in_hbm(jnp.transpose(wigner[0], (1, 0, 2))), in_hbm(radial[0]),
    )

    came = after(came, pick)
    held = jnp.concatenate([held, came], axis=0)
    held, feats_far = lax.optimization_barrier((held, feats_far))
    near, up = bits - 2, bits - 3
    pieces = {0: held, 1 << near: swap(held, near), 1 << up: swap(held, up)}

    keeps_sends = pl.pallas_call(
        grad_kernel,
        out_shape=[
            kind((2,) * (bits - 1) + (rows, LANES), dtype)
            for kind, dtype in ((pltpu.VMEM, F32), (jax.ShapeDtypeStruct, BF16))
            for rows in split
        ],
        in_specs=[spec()] * 9,
        out_specs=[spec()] * 4,
        scratch_shapes=[
            picked_scratch,
            pltpu.VMEM((5 * channels, edges), BF16),
            pltpu.VMEM((4 * channels, 2 * edges), BF16),
            pltpu.VMEM((3 * channels, 2 * edges), BF16),
            pltpu.VMEM((total_rows, LANES), F32),
        ],
        compiler_params=limit(17),
        cost_estimate=cost(KCOST, KCOST),
        name="gradients",
    )(feats_core, feats_near, feats_far, rot, gate, pick, *bmats)
    keeps, sends = keeps_sends[:2], list(keeps_sends[2:])
    *sends, pieces[1 << near], pieces[1 << up] = lax.optimization_barrier(
        (*sends, pieces[1 << near], pieces[1 << up])
    )
    pieces[1 << near | 1 << up] = swap(pieces[1 << near], up)

    low_to_high = list(range(1, bits))
    orders = [low_to_high, low_to_high[1:] + low_to_high[:1]]
    left = [list(reversed(low_to_high)) for _ in orders]

    def halve(turn, keeps, cames):
        stays, aways = [], []
        for part, (keep, came) in enumerate(zip(keeps, cames)):
            bit = orders[part][turn]
            axis = left[part].index(bit)
            left[part].remove(bit)
            shape = (2,) * len(left[part]) + came.shape[-2:]
            stay, away = pl.pallas_call(
                functools.partial(halve_kernel, axis, bit),
                out_shape=[pltpu.VMEM(shape, F32), jax.ShapeDtypeStruct(shape, BF16)],
                in_specs=[spec()] * 2,
                out_specs=[spec()] * 2,
                compiler_params=limit(6),
                cost_estimate=cost(KCOST, KCOST),
                name="halve",
            )(keep, came)
            stays.append(stay)
            aways.append(away)
        return stays, aways

    def exchange(turn, aways):
        return [swap(away, orders[part][turn]) for part, away in enumerate(aways)]

    stays, aways = halve(0, keeps, [swap(send, 0) for send in sends])

    def fan_out(some):
        some = dict(some)
        for bit in reversed(range(up)):
            some.update({mask | 1 << bit: swap(some[mask], bit) for mask in list(some)})
        return some

    last = pieces.pop(1 << near | 1 << up)
    pieces = fan_out(pieces)
    cames = exchange(0, aways)
    for turn in range(1, bits - 1):
        stays, aways = halve(turn, stays, cames)
        masks = list(pieces)
        together = lax.optimization_barrier((*aways, *pieces.values()))
        aways, pieces = together[:2], dict(zip(masks, together[2:]))
        if turn == bits - 2:
            pieces.update(fan_out({1 << near | 1 << up: after(last, *aways)}))
        cames = exchange(turn, aways)

    masks = list(pieces)
    ready = list(pieces.values())
    grads_core, grads_own, grads_far = pl.pallas_call(
        functools.partial(backward_kernel, masks, 1 << (bits - 1)),
        out_shape=[
            jax.ShapeDtypeStruct((coefs, atoms, channels), kind) for kind in (BF16, F32, BF16)
        ],
        in_specs=[spec()] * (6 + len(masks)),
        out_specs=[spec()] * 3,
        scratch_shapes=[pltpu.VMEM((total_rows, LANES), F32)]
        + [pltpu.VMEM((g * channels, g * channels), BF16) for g in WEIGHTS]
        + [
            pltpu.VMEM((19, channels, edges), F32),
            pltpu.VMEM((coefs, channels, edges), BF16),
        ],
        compiler_params=limit(18),
        cost_estimate=cost(KCOST, KCOST),
        name="backward",
    )(*ready[: len(masks)], *bmats, rot, gate, pick)
    total = grads_own + swap(grads_core, 0).astype(F32) + across(grads_far).astype(F32)
    atom_grads = jnp.transpose(total, (1, 0, 2))[None]

    cames = lax.optimization_barrier((*cames, grads_own))[:2]
    systems = lax.axis_size("dp")
    shares, roundeds = [], []
    for stay, came in zip(stays, cames):
        share, rounded = pl.pallas_call(
            finish_kernel,
            out_shape=[pltpu.VMEM(came.shape, F32), jax.ShapeDtypeStruct(came.shape, BF16)],
            in_specs=[spec()] * 2,
            out_specs=[spec()] * 2,
            compiler_params=limit(6),
            cost_estimate=cost(KCOST, KCOST),
            name="finish",
        )(stay, came)
        shares.append(share)
        roundeds.append(rounded)

    own_experts = mixing.shape[1] // systems
    expert_part = None
    for first_row, share, rounded in reversed(list(zip((0, rows_a), shares, roundeds))):
        others = [
            lax.ppermute(rounded, "dp", [(i, (i + n) % systems) for i in range(systems)])
            for n in range(1, systems)
        ]
        rows = share.shape[0]
        before = [] if expert_part is None else [expert_part]
        expert_part = pl.pallas_call(
            functools.partial(expert_kernel, first_row),
            out_shape=jax.ShapeDtypeStruct((own_experts, shard_rows * LANES), F32),
            in_specs=[spec()] * (1 + systems) + [spec(pl.ANY)] * len(before),
            out_specs=spec(pl.ANY),
            input_output_aliases={1 + systems: 0} if before else {},
            scratch_shapes=[
                pltpu.VMEM((max(systems - 1, 1), rows, LANES), F32),
                pltpu.VMEM((own_experts, rows * LANES), F32),
                pltpu.SemaphoreType.DMA((2,)),
            ],
            compiler_params=limit(4),
            cost_estimate=cost(KCOST, KCOST),
            name="experts",
        )(mixing, share, *others, *before)
    return (atom_grads, expert_part)


def solution(mesh):
    in_specs = (
        P("dp", "graph", None, None),
        P("dp", "graph", None, None),
        P("dp", None, None, "graph"),
        P("dp", "graph", None),
        P("dp", "graph"),
        P("dp", "graph"),
        P("dp", "graph"),
        P("dp", "graph"),
        P(),
    )
    out_specs = (P("dp", "graph", None, None), P("dp", "graph"))
    return jax.shard_map(
        on_device, mesh=mesh, in_specs=in_specs, out_specs=out_specs, check_vma=False
    )
```

```python
import functools
import itertools

import jax
import jax.numpy as jnp
from jax import lax
from jax.experimental import pallas as pl
from jax.experimental.pallas import tpu as pltpu
from jax.sharding import PartitionSpec as P

BF16 = jnp.bfloat16
F32 = jnp.float32
LANES = 128
GROUPS = ((0, 5), (5, 9), (9, 13), (13, 16), (16, 19))
FRAME_ROWS = tuple(
    tuple(
        first + degree - order
        for first, order in ((0, 0), (5, 1), (9, 1), (13, 2), (16, 2))
        if degree >= order
    )
    for degree in range(5)
)
NODE_COLS = tuple(tuple(range(l * l, (l + 1) * (l + 1))) for l in range(5))
WEIGHTS = (5, 4, 4, 3, 3)


def first_rows():
    rows, out = 0, []
    for group_rows in WEIGHTS:
        out.append(rows)
        rows += group_rows * group_rows * LANES
    return out


def place(row):
    if row < 5:
        return 0, row, 0
    if row < 13:
        return 1, (row - 5) % 4, (row - 5) // 4
    return 2, (row - 13) % 3, (row - 13) // 3


def for_chunks(channels, edges, size, body):
    for edge_first in range(0, edges, LANES):

        def step(turn, unused, edge_first=edge_first):
            body(pl.multiple_of(turn * size, size), edge_first)
            return unused

        lax.fori_loop(0, channels // size, step, 0)


def nt(left, right):
    return lax.dot_general(left, right, (((1,), (1,)), ((), ())), preferred_element_type=F32)


def tn(left, right):
    return lax.dot_general(left, right, (((0,), (0,)), ((), ())), preferred_element_type=F32)


def one_hot(count, wanted):
    edges = wanted.shape[1]
    hit = lax.broadcasted_iota(jnp.int32, (count, edges), 0) == wanted
    return hit.astype(F32).astype(BF16)


def near_pick(source, atoms):
    index = lax.axis_index("graph")
    shard = lax.div(source[...], atoms)
    slot = jnp.where(shard == index, 1, jnp.where(shard == (index ^ 1), 0, 2))
    return one_hot(3 * atoms, (slot - shard) * atoms + source[...])


def gather(pieces, pick, picked):
    for coef in range(picked.shape[0]):
        parts = [piece[coef].astype(F32) for piece in pieces]
        block = parts[0] if len(parts) == 1 else jnp.concatenate(parts, axis=0)
        picked[coef] = tn(block.astype(BF16), pick)


def rotate(rot, picked, emit):
    channels, edges = picked.shape[1:]

    def body(at, edge_first):
        lanes = slice(edge_first, edge_first + LANES)
        for rows, cols in zip(FRAME_ROWS, NODE_COLS):
            totals = [None] * len(rows)
            for col in cols:
                value = picked[col, pl.ds(at, 32), lanes]
                for n, row in enumerate(rows):
                    term = rot[col, row : row + 1, lanes] * value
                    totals[n] = term if totals[n] is None else totals[n] + term
            for row, total in zip(rows, totals):
                emit(row, at, edge_first, total)

    for_chunks(channels, edges, 32, body)


def cot_kernel(
    source, target, counts, cot, feats, wigner, radial,
    b0, b1, b2, rot, gate, pick, feats_near,
    source_v, target_v, cot_v, wigner_v, radial_v, sems, picked,
):
    pairs = (
        (target, target_v), (cot, cot_v), (wigner, wigner_v), (radial, radial_v),
        (source, source_v), (feats, feats_near),
    )
    copies = [pltpu.make_async_copy(*pair, sems.at[n]) for n, pair in enumerate(pairs)]
    for copy in copies:
        copy.start()
    atoms, channels = cot.shape[1:]
    edges = target.shape[1]
    copies[0].wait()
    copies[1].wait()
    bmat = (b0, b1, b2)
    live = lax.broadcasted_iota(jnp.int32, (1, edges), 1) < counts[0, 0]
    gather((cot_v,), one_hot(atoms, jnp.where(live, target_v[...], -1)), picked)
    copies[2].wait()
    rot[...] = wigner_v[...].astype(F32)

    def emit(row, at, edge_first, total):
        which, block, half = place(row)
        rows = pl.ds(pl.multiple_of(block * channels + at, 32), 32)
        lanes = slice(half * edges + edge_first, half * edges + edge_first + LANES)
        bmat[which][rows, lanes] = total.astype(BF16)

    rotate(rot, picked, emit)
    for copy in copies[3:]:
        copy.wait()
    gate[...] = radial_v[...].astype(F32).T
    pick[...] = near_pick(source_v, atoms)


def grad_kernel(
    feats_core, feats_own, feats_far, rot, gate, pick, b0, b1, b2,
    keep_a, keep_b, send_a, send_b,
    picked, a0, a1, a2, grad,
):
    channels, edges = gate.shape
    amat = (a0, a1, a2)
    gather((feats_core, feats_own, feats_far), pick[...], picked)

    def emit(row, at, edge_first, total):
        which, block, half = place(row)
        rows = pl.ds(pl.multiple_of(block * channels + at, 32), 32)
        gated = total * gate[pl.ds(at, 32), edge_first : edge_first + LANES]
        lanes = slice(half * edges + edge_first, half * edges + edge_first + LANES)
        amat[which][rows, lanes] = gated.astype(BF16)

    rotate(rot, picked, emit)

    def put(first, blocks, block, product):
        for n in range(product.shape[1] // LANES):
            grad[pl.ds(first + block + n, blocks * LANES, stride=blocks), :] = product[
                :, n * LANES : (n + 1) * LANES
            ]

    firsts = first_rows()
    for order, (left, right) in enumerate(((a0, b0), (a1, b1), (a2, b2))):
        blocks = 5 - order
        first = firsts[max(2 * order - 1, 0)]
        for block in range(0, blocks, 2):
            width = min(2, blocks - block)
            part = right[block * LANES : (block + width) * LANES, :]
            put(first, blocks, block, nt(left[...], part))
            if order:
                product = nt(left[:, :edges], part[:, edges:]) - nt(left[:, edges:], part[:, :edges])
                put(firsts[2 * order], blocks, block, product)
    rows_a, rows_b = keep_a.shape[-2], keep_b.shape[-2]
    rows = rows_a + rows_b
    parity = lax.rem(lax.axis_index("graph"), 2)
    for n, spot in enumerate(spots(keep_a)):
        at = (2 * n + 1 - parity) * rows
        send_a[spot] = grad[pl.ds(at, rows_a), :].astype(BF16)
        send_b[spot] = grad[pl.ds(at + rows_a, rows_b), :].astype(BF16)
        at = (2 * n + parity) * rows
        keep_a[spot] = grad[pl.ds(at, rows_a), :]
        keep_b[spot] = grad[pl.ds(at + rows_a, rows_b), :]


def unroll_kernel(flat, out, line, wide, sem):
    copy = pltpu.make_async_copy(flat, line, sem)
    copy.start()
    copy.wait()
    rows = out.shape[1]
    for row in range(rows):
        wide[row : row + 1, :] = line[:, row * LANES : (row + 1) * LANES].astype(F32)
    out[0] = wide[...].astype(BF16)


def spots(ref):
    return itertools.product(*(range(n) for n in ref.shape[:-2]))


def halve_kernel(axis, bit, keep, came, stay, away):
    side = (lax.axis_index("graph") >> bit) & 1
    for spot in spots(stay):
        here = (*spot[:axis], side, *spot[axis:])
        there = (*spot[:axis], 1 - side, *spot[axis:])
        at = spot or Ellipsis
        stay[at] = keep[here] + came[here].astype(F32)
        away[at] = (keep[there] + came[there].astype(F32)).astype(BF16)


def finish_kernel(keep, came, share, rounded):
    total = keep[...] + came[...].astype(F32)
    share[...] = total
    rounded[...] = total.astype(BF16)


def backward_kernel(masks, high, *refs):
    pieces, refs = refs[: len(masks)], refs[len(masks) :]
    b0, b1, b2, rot, gate, pick, out_core, out_own, out_far = refs[:9]
    flat, w0, w1r, w1i, w2r, w2i, back, spread = refs[9:]
    coefs, atoms, channels = out_own.shape
    edges = gate.shape[1]
    index = lax.axis_index("graph")
    rows = pieces[0].shape[1]
    for mask, piece in zip(masks, pieces):
        for n in range(2):
            shard = index ^ (mask + n * high)
            flat[pl.ds(shard * rows, rows), :] = piece[n].astype(F32)
    for matrix, blocks, first in zip((w0, w1r, w1i, w2r, w2i), WEIGHTS, first_rows()):
        for block in range(blocks):
            matrix[:, block * LANES : (block + 1) * LANES] = flat[
                pl.ds(first + block, blocks * LANES, stride=blocks), :
            ].astype(BF16)

    dot = functools.partial(jnp.dot, preferred_element_type=F32)
    for row in range(5):
        rows = slice(row * channels, (row + 1) * channels)
        back[row] = dot(w0[rows, :], b0[...]) * gate[...]
    for first, real, imag, both, blocks in ((5, w1r, w1i, b1, 4), (13, w2r, w2i, b2, 3)):
        for block in range(blocks):
            rows = slice(block * channels, (block + 1) * channels)
            straight = dot(real[rows, :], both[...])
            crossed = dot(imag[rows, :], both[...])
            back[first + block] = (straight[:, :edges] + crossed[:, edges:]) * gate[...]
            back[first + blocks + block] = (straight[:, edges:] - crossed[:, :edges]) * gate[...]

    def body(at, edge_first):
        lanes = slice(edge_first, edge_first + LANES)
        for rows, cols in zip(FRAME_ROWS, NODE_COLS):
            totals = [None] * len(cols)
            for row in rows:
                value = back[row, pl.ds(at, 16), lanes]
                for n, col in enumerate(cols):
                    term = rot[col, row : row + 1, lanes] * value
                    totals[n] = term if totals[n] is None else totals[n] + term
            for col, total in zip(cols, totals):
                spread[col, pl.ds(at, 16), lanes] = total.astype(BF16)

    for_chunks(channels, edges, 16, body)
    for col in range(coefs):
        block = nt(pick[...], spread[col])
        out_core[col] = block[:atoms].astype(BF16)
        out_own[col] = block[atoms : 2 * atoms]
        out_far[col] = block[2 * atoms :].astype(BF16)


def expert_kernel(first_row, mixing, own_rows, *refs):
    systems, experts_all = mixing.shape
    others, (out, wide, block, sems) = refs[: systems - 1], refs[-4:]
    experts = out.shape[0]
    rows = own_rows.shape[0]
    position = lax.axis_index("dp")
    for n, other in enumerate(others):
        wide[n] = other[...].astype(F32)
    spot = lax.broadcasted_iota(jnp.int32, (experts, experts_all), 1)
    mine = lax.broadcasted_iota(jnp.int32, (experts, experts_all), 0) + position * experts
    scales = []
    for n in range(systems):
        system = lax.rem(position - n + systems, systems)
        row = mixing[pl.ds(system, 1), :]
        column = jnp.sum(jnp.where(spot == mine, row, 0.0), axis=1, keepdims=True)
        scales.append(jnp.broadcast_to(column, (experts, LANES)))
    chunk = rows // 2
    group = max(g for g in range(1, 9) if chunk % g == 0)
    copies = []
    for part in range(2):

        def step(turn, unused, part=part):
            for n in range(group):
                at = part * chunk + turn * group + n
                total = own_rows[pl.ds(at, 1), :] * scales[0]
                for other in range(systems - 1):
                    total = total + wide[other, pl.ds(at, 1), :] * scales[other + 1]
                block[:, pl.ds(pl.multiple_of(at * LANES, LANES), LANES)] = total
            return unused

        lax.fori_loop(0, chunk // group, step, 0)
        here = slice(part * chunk * LANES, (part + 1) * chunk * LANES)
        there = slice(here.start + first_row * LANES, here.stop + first_row * LANES)
        copy = pltpu.make_async_copy(block.at[:, here], out.at[:, there], sems.at[part])
        copy.start()
        copies.append(copy)
    for copy in copies:
        copy.wait()


def spec(space=pltpu.VMEM):
    return pl.BlockSpec(memory_space=space)


KCOST = 1000


def limit(mebibytes):
    return pltpu.CompilerParams(vmem_limit_bytes=mebibytes * 1024 * 1024)


def cost(flops, size):
    return pl.CostEstimate(flops=flops, bytes_accessed=size, transcendentals=0)


def swap(x, bit):
    size = lax.axis_size("graph")
    return lax.ppermute(x, "graph", [(i, i ^ (1 << bit)) for i in range(size)])


def across(x):
    size = lax.axis_size("graph")
    pairs = [(i, i + 1) for i in range(1, size - 1, 2)]
    return lax.ppermute(x, "graph", pairs + [(j, i) for i, j in pairs])


def in_hbm(x):
    return pltpu.with_memory_space_constraint(x, pltpu.HBM)


def after(x, *others):
    return lax.optimization_barrier((x,) + others)[0]


def on_device(
    node_feats, node_cot, wigner, radial, source_atom, target_index, edge_counts,
    merged_weights, mixing,
):
    atoms, coefs, channels = node_feats.shape[1:]
    edges = source_atom.shape[1]
    size = lax.axis_size("graph")
    bits = size.bit_length() - 1
    shard_rows = merged_weights.shape[1] // LANES
    total_rows = shard_rows * size
    rows_a = (shard_rows // 2 + 7) // 8 * 8
    split = (rows_a, shard_rows - rows_a)

    feats = jnp.transpose(node_feats[0], (1, 0, 2))
    feats_far = across(feats)
    feats_core = swap(feats, 0)
    target, feats_core = lax.optimization_barrier((target_index, feats_core))

    held = pl.pallas_call(
        unroll_kernel,
        out_shape=jax.ShapeDtypeStruct((1, shard_rows, LANES), BF16),
        in_specs=[spec(pltpu.HBM)],
        out_specs=spec(),
        scratch_shapes=[
            pltpu.VMEM(merged_weights.shape, BF16),
            pltpu.VMEM((shard_rows, LANES), F32),
            pltpu.SemaphoreType.DMA,
        ],
        compiler_params=limit(6),
        cost_estimate=cost(KCOST, KCOST),
        name="rows",
    )(in_hbm(merged_weights))
    came = swap(held, bits - 1)

    hbm = spec(pltpu.HBM)
    picked_scratch = pltpu.VMEM((coefs, channels, edges), F32)
    *bmats, rot, gate, pick, feats_near = pl.pallas_call(
        cot_kernel,
        out_shape=[
            pltpu.VMEM((5 * channels, edges), BF16),
            pltpu.VMEM((4 * channels, 2 * edges), BF16),
            pltpu.VMEM((3 * channels, 2 * edges), BF16),
            pltpu.VMEM((coefs, 19, edges), F32),
            pltpu.VMEM((channels, edges), F32),
            jax.ShapeDtypeStruct((3 * atoms, edges), BF16),
            pltpu.VMEM((coefs, atoms, channels), BF16),
        ],
        in_specs=[hbm, hbm, spec(pltpu.SMEM), hbm, hbm, hbm, hbm],
        out_specs=[spec()] * 7,
        scratch_shapes=[
            pltpu.VMEM((1, edges), jnp.int32),
            pltpu.VMEM((1, edges), jnp.int32),
            pltpu.VMEM((coefs, atoms, channels), BF16),
            pltpu.VMEM((coefs, 19, edges), BF16),
            pltpu.VMEM((edges, channels), BF16),
            pltpu.SemaphoreType.DMA((6,)),
            picked_scratch,
        ],
        compiler_params=limit(12),
        cost_estimate=cost(KCOST, KCOST),
        name="cotangents",
    )(
        in_hbm(source_atom), in_hbm(target), edge_counts,
        in_hbm(jnp.transpose(node_cot[0], (1, 0, 2))), in_hbm(feats),
        in_hbm(jnp.transpose(wigner[0], (1, 0, 2))), in_hbm(radial[0]),
    )

    came = after(came, pick)
    held = jnp.concatenate([held, came], axis=0)
    held, feats_far = lax.optimization_barrier((held, feats_far))
    near, up = bits - 2, bits - 3
    pieces = {0: held, 1 << near: swap(held, near), 1 << up: swap(held, up)}

    keeps_sends = pl.pallas_call(
        grad_kernel,
        out_shape=[
            kind((2,) * (bits - 1) + (rows, LANES), dtype)
            for kind, dtype in ((pltpu.VMEM, F32), (jax.ShapeDtypeStruct, BF16))
            for rows in split
        ],
        in_specs=[spec()] * 9,
        out_specs=[spec()] * 4,
        scratch_shapes=[
            picked_scratch,
            pltpu.VMEM((5 * channels, edges), BF16),
            pltpu.VMEM((4 * channels, 2 * edges), BF16),
            pltpu.VMEM((3 * channels, 2 * edges), BF16),
            pltpu.VMEM((total_rows, LANES), F32),
        ],
        compiler_params=limit(17),
        cost_estimate=cost(KCOST, KCOST),
        name="gradients",
    )(feats_core, feats_near, feats_far, rot, gate, pick, *bmats)
    keeps, sends = keeps_sends[:2], list(keeps_sends[2:])
    *sends, pieces[1 << near], pieces[1 << up] = lax.optimization_barrier(
        (*sends, pieces[1 << near], pieces[1 << up])
    )
    pieces[1 << near | 1 << up] = swap(pieces[1 << near], up)

    low_to_high = list(range(1, bits))
    orders = [low_to_high, low_to_high[1:] + low_to_high[:1]]
    left = [list(reversed(low_to_high)) for _ in orders]

    def halve(turn, keeps, cames):
        stays, aways = [], []
        for part, (keep, came) in enumerate(zip(keeps, cames)):
            bit = orders[part][turn]
            axis = left[part].index(bit)
            left[part].remove(bit)
            shape = (2,) * len(left[part]) + came.shape[-2:]
            stay, away = pl.pallas_call(
                functools.partial(halve_kernel, axis, bit),
                out_shape=[pltpu.VMEM(shape, F32), jax.ShapeDtypeStruct(shape, BF16)],
                in_specs=[spec()] * 2,
                out_specs=[spec()] * 2,
                compiler_params=limit(6),
                cost_estimate=cost(KCOST, KCOST),
                name="halve",
            )(keep, came)
            stays.append(stay)
            aways.append(away)
        return stays, aways

    def exchange(turn, aways):
        return [swap(away, orders[part][turn]) for part, away in enumerate(aways)]

    stays, aways = halve(0, keeps, [swap(send, 0) for send in sends])

    def fan_out(some):
        some = dict(some)
        for bit in reversed(range(up)):
            some.update({mask | 1 << bit: swap(some[mask], bit) for mask in list(some)})
        return some

    last = pieces.pop(1 << near | 1 << up)
    pieces = fan_out(pieces)
    cames = exchange(0, aways)
    for turn in range(1, bits - 1):
        stays, aways = halve(turn, stays, cames)
        masks = list(pieces)
        together = lax.optimization_barrier((*aways, *pieces.values()))
        aways, pieces = together[:2], dict(zip(masks, together[2:]))
        if turn == bits - 2:
            pieces.update(fan_out({1 << near | 1 << up: after(last, *aways)}))
        cames = exchange(turn, aways)

    masks = list(pieces)
    ready = list(pieces.values())
    grads_core, grads_own, grads_far = pl.pallas_call(
        functools.partial(backward_kernel, masks, 1 << (bits - 1)),
        out_shape=[
            jax.ShapeDtypeStruct((coefs, atoms, channels), kind) for kind in (BF16, F32, BF16)
        ],
        in_specs=[spec()] * (6 + len(masks)),
        out_specs=[spec()] * 3,
        scratch_shapes=[pltpu.VMEM((total_rows, LANES), F32)]
        + [pltpu.VMEM((g * channels, g * channels), BF16) for g in WEIGHTS]
        + [
            pltpu.VMEM((19, channels, edges), F32),
            pltpu.VMEM((coefs, channels, edges), BF16),
        ],
        compiler_params=limit(18),
        cost_estimate=cost(KCOST, KCOST),
        name="backward",
    )(*ready[: len(masks)], *bmats, rot, gate, pick)
    total = grads_own + swap(grads_core, 0).astype(F32) + across(grads_far).astype(F32)
    atom_grads = jnp.transpose(total, (1, 0, 2))[None]

    cames = lax.optimization_barrier((*cames, grads_own))[:2]
    systems = lax.axis_size("dp")
    shares, roundeds = [], []
    for stay, came in zip(stays, cames):
        share, rounded = pl.pallas_call(
            finish_kernel,
            out_shape=[pltpu.VMEM(came.shape, F32), jax.ShapeDtypeStruct(came.shape, BF16)],
            in_specs=[spec()] * 2,
            out_specs=[spec()] * 2,
            compiler_params=limit(6),
            cost_estimate=cost(KCOST, KCOST),
            name="finish",
        )(stay, came)
        shares.append(share)
        roundeds.append(rounded)

    own_experts = mixing.shape[1] // systems
    expert_part = None
    for first_row, share, rounded in reversed(list(zip((0, rows_a), shares, roundeds))):
        others = [
            lax.ppermute(rounded, "dp", [(i, (i + n) % systems) for i in range(systems)])
            for n in range(1, systems)
        ]
        rows = share.shape[0]
        before = [] if expert_part is None else [expert_part]
        expert_part = pl.pallas_call(
            functools.partial(expert_kernel, first_row),
            out_shape=jax.ShapeDtypeStruct((own_experts, shard_rows * LANES), F32),
            in_specs=[spec()] * (1 + systems) + [spec(pl.ANY)] * len(before),
            out_specs=spec(pl.ANY),
            input_output_aliases={1 + systems: 0} if before else {},
            scratch_shapes=[
                pltpu.VMEM((max(systems - 1, 1), rows, LANES), F32),
                pltpu.VMEM((own_experts, rows * LANES), F32),
                pltpu.SemaphoreType.DMA((2,)),
            ],
            compiler_params=limit(4),
            cost_estimate=cost(KCOST, KCOST),
            name="experts",
        )(mixing, share, *others, *before)
    return (atom_grads, expert_part)


def solution(mesh):
    in_specs = (
        P("dp", "graph", None, None),
        P("dp", "graph", None, None),
        P("dp", None, None, "graph"),
        P("dp", "graph", None),
        P("dp", "graph"),
        P("dp", "graph"),
        P("dp", "graph"),
        P("dp", "graph"),
        P(),
    )
    out_specs = (P("dp", "graph", None, None), P("dp", "graph"))
    return jax.shard_map(
        on_device, mesh=mesh, in_specs=in_specs, out_specs=out_specs, check_vma=False
    )
```

```python
import functools
import itertools

import jax
import jax.numpy as jnp
from jax import lax
from jax.experimental import pallas as pl
from jax.experimental.pallas import tpu as pltpu
from jax.sharding import PartitionSpec as P

BF16 = jnp.bfloat16
F32 = jnp.float32
LANES = 128
GROUPS = ((0, 5), (5, 9), (9, 13), (13, 16), (16, 19))
FRAME_ROWS = tuple(
    tuple(
        first + degree - order
        for first, order in ((0, 0), (5, 1), (9, 1), (13, 2), (16, 2))
        if degree >= order
    )
    for degree in range(5)
)
NODE_COLS = tuple(tuple(range(l * l, (l + 1) * (l + 1))) for l in range(5))
WEIGHTS = (5, 4, 4, 3, 3)


def first_rows():
    rows, out = 0, []
    for group_rows in WEIGHTS:
        out.append(rows)
        rows += group_rows * group_rows * LANES
    return out


def place(row):
    if row < 5:
        return 0, row, 0
    if row < 13:
        return 1, (row - 5) % 4, (row - 5) // 4
    return 2, (row - 13) % 3, (row - 13) // 3


def for_chunks(channels, edges, size, body):
    for edge_first in range(0, edges, LANES):

        def step(turn, unused, edge_first=edge_first):
            body(pl.multiple_of(turn * size, size), edge_first)
            return unused

        lax.fori_loop(0, channels // size, step, 0)


def nt(left, right):
    return lax.dot_general(left, right, (((1,), (1,)), ((), ())), preferred_element_type=F32)


def tn(left, right):
    return lax.dot_general(left, right, (((0,), (0,)), ((), ())), preferred_element_type=F32)


def one_hot(count, wanted):
    edges = wanted.shape[1]
    hit = lax.broadcasted_iota(jnp.int32, (count, edges), 0) == wanted
    return hit.astype(F32).astype(BF16)


def near_pick(source, atoms):
    index = lax.axis_index("graph")
    shard = lax.div(source[...], atoms)
    slot = jnp.where(shard == index, 1, jnp.where(shard == (index ^ 1), 0, 2))
    return one_hot(3 * atoms, (slot - shard) * atoms + source[...])


def gather(pieces, pick, picked):
    for coef in range(picked.shape[0]):
        parts = [piece[coef].astype(F32) for piece in pieces]
        block = parts[0] if len(parts) == 1 else jnp.concatenate(parts, axis=0)
        picked[coef] = tn(block.astype(BF16), pick)


def rotate(rot, picked, emit):
    channels, edges = picked.shape[1:]

    def body(at, edge_first):
        lanes = slice(edge_first, edge_first + LANES)
        for rows, cols in zip(FRAME_ROWS, NODE_COLS):
            totals = [None] * len(rows)
            for col in cols:
                value = picked[col, pl.ds(at, 32), lanes]
                for n, row in enumerate(rows):
                    term = rot[col, row : row + 1, lanes] * value
                    totals[n] = term if totals[n] is None else totals[n] + term
            for row, total in zip(rows, totals):
                emit(row, at, edge_first, total)

    for_chunks(channels, edges, 32, body)


def cot_kernel(
    source, target, counts, cot, feats, wigner, radial,
    b0, b1, b2, rot, gate, pick, feats_near,
    source_v, target_v, cot_v, wigner_v, radial_v, sems, picked,
):
    pairs = (
        (target, target_v), (cot, cot_v), (wigner, wigner_v), (radial, radial_v),
        (source, source_v), (feats, feats_near),
    )
    copies = [pltpu.make_async_copy(*pair, sems.at[n]) for n, pair in enumerate(pairs)]
    for copy in copies:
        copy.start()
    atoms, channels = cot.shape[1:]
    edges = target.shape[1]
    copies[0].wait()
    copies[1].wait()
    bmat = (b0, b1, b2)
    live = lax.broadcasted_iota(jnp.int32, (1, edges), 1) < counts[0, 0]
    gather((cot_v,), one_hot(atoms, jnp.where(live, target_v[...], -1)), picked)
    copies[2].wait()
    rot[...] = wigner_v[...].astype(F32)

    def emit(row, at, edge_first, total):
        which, block, half = place(row)
        rows = pl.ds(pl.multiple_of(block * channels + at, 32), 32)
        lanes = slice(half * edges + edge_first, half * edges + edge_first + LANES)
        bmat[which][rows, lanes] = total.astype(BF16)

    rotate(rot, picked, emit)
    for copy in copies[3:]:
        copy.wait()
    gate[...] = radial_v[...].astype(F32).T
    pick[...] = near_pick(source_v, atoms)


def grad_kernel(
    feats_core, feats_own, feats_far, rot, gate, pick, b0, b1, b2,
    keep_a, keep_b, send_a, send_b,
    picked, a0, a1, a2, grad,
):
    channels, edges = gate.shape
    amat = (a0, a1, a2)
    gather((feats_core, feats_own, feats_far), pick[...], picked)

    def emit(row, at, edge_first, total):
        which, block, half = place(row)
        rows = pl.ds(pl.multiple_of(block * channels + at, 32), 32)
        gated = total * gate[pl.ds(at, 32), edge_first : edge_first + LANES]
        lanes = slice(half * edges + edge_first, half * edges + edge_first + LANES)
        amat[which][rows, lanes] = gated.astype(BF16)

    rotate(rot, picked, emit)

    def put(first, blocks, block, product):
        for n in range(product.shape[1] // LANES):
            grad[pl.ds(first + block + n, blocks * LANES, stride=blocks), :] = product[
                :, n * LANES : (n + 1) * LANES
            ]

    firsts = first_rows()
    for order, (left, right) in enumerate(((a0, b0), (a1, b1), (a2, b2))):
        blocks = 5 - order
        first = firsts[max(2 * order - 1, 0)]
        for block in range(0, blocks, 2):
            width = min(2, blocks - block)
            part = right[block * LANES : (block + width) * LANES, :]
            put(first, blocks, block, nt(left[...], part))
            if order:
                product = nt(left[:, :edges], part[:, edges:]) - nt(left[:, edges:], part[:, :edges])
                put(firsts[2 * order], blocks, block, product)
    rows_a, rows_b = keep_a.shape[-2], keep_b.shape[-2]
    rows = rows_a + rows_b
    parity = lax.rem(lax.axis_index("graph"), 2)
    for n, spot in enumerate(spots(keep_a)):
        at = (2 * n + 1 - parity) * rows
        send_a[spot] = grad[pl.ds(at, rows_a), :].astype(BF16)
        send_b[spot] = grad[pl.ds(at + rows_a, rows_b), :].astype(BF16)
        at = (2 * n + parity) * rows
        keep_a[spot] = grad[pl.ds(at, rows_a), :]
        keep_b[spot] = grad[pl.ds(at + rows_a, rows_b), :]


def unroll_kernel(flat, out, line, wide, sem):
    copy = pltpu.make_async_copy(flat, line, sem)
    copy.start()
    copy.wait()
    rows = out.shape[1]
    for row in range(rows):
        wide[row : row + 1, :] = line[:, row * LANES : (row + 1) * LANES].astype(F32)
    out[0] = wide[...].astype(BF16)


def spots(ref):
    return itertools.product(*(range(n) for n in ref.shape[:-2]))


def halve_kernel(axis, bit, keep, came, stay, away):
    side = (lax.axis_index("graph") >> bit) & 1
    for spot in spots(stay):
        here = (*spot[:axis], side, *spot[axis:])
        there = (*spot[:axis], 1 - side, *spot[axis:])
        at = spot or Ellipsis
        stay[at] = keep[here] + came[here].astype(F32)
        away[at] = (keep[there] + came[there].astype(F32)).astype(BF16)


def finish_kernel(keep, came, share, rounded):
    total = keep[...] + came[...].astype(F32)
    share[...] = total
    rounded[...] = total.astype(BF16)


def backward_kernel(masks, high, *refs):
    pieces, refs = refs[: len(masks)], refs[len(masks) :]
    b0, b1, b2, rot, gate, pick, out_core, out_own, out_far = refs[:9]
    flat, w0, w1r, w1i, w2r, w2i, back, spread = refs[9:]
    coefs, atoms, channels = out_own.shape
    edges = gate.shape[1]
    index = lax.axis_index("graph")
    rows = pieces[0].shape[1]
    for mask, piece in zip(masks, pieces):
        for n in range(2):
            shard = index ^ (mask + n * high)
            flat[pl.ds(shard * rows, rows), :] = piece[n].astype(F32)
    for matrix, blocks, first in zip((w0, w1r, w1i, w2r, w2i), WEIGHTS, first_rows()):
        for block in range(blocks):
            matrix[:, block * LANES : (block + 1) * LANES] = flat[
                pl.ds(first + block, blocks * LANES, stride=blocks), :
            ].astype(BF16)

    dot = functools.partial(jnp.dot, preferred_element_type=F32)
    for row in range(5):
        rows = slice(row * channels, (row + 1) * channels)
        back[row] = dot(w0[rows, :], b0[...]) * gate[...]
    for first, real, imag, both, blocks in ((5, w1r, w1i, b1, 4), (13, w2r, w2i, b2, 3)):
        for block in range(blocks):
            rows = slice(block * channels, (block + 1) * channels)
            straight = dot(real[rows, :], both[...])
            crossed = dot(imag[rows, :], both[...])
            back[first + block] = (straight[:, :edges] + crossed[:, edges:]) * gate[...]
            back[first + blocks + block] = (straight[:, edges:] - crossed[:, :edges]) * gate[...]

    def body(at, edge_first):
        lanes = slice(edge_first, edge_first + LANES)
        for rows, cols in zip(FRAME_ROWS, NODE_COLS):
            totals = [None] * len(cols)
            for row in rows:
                value = back[row, pl.ds(at, 16), lanes]
                for n, col in enumerate(cols):
                    term = rot[col, row : row + 1, lanes] * value
                    totals[n] = term if totals[n] is None else totals[n] + term
            for col, total in zip(cols, totals):
                spread[col, pl.ds(at, 16), lanes] = total.astype(BF16)

    for_chunks(channels, edges, 16, body)
    for col in range(coefs):
        block = nt(pick[...], spread[col])
        out_core[col] = block[:atoms].astype(BF16)
        out_own[col] = block[atoms : 2 * atoms]
        out_far[col] = block[2 * atoms :].astype(BF16)


def expert_kernel(first_row, mixing, own_rows, *refs):
    systems, experts_all = mixing.shape
    others, (out, wide, block, sems) = refs[: systems - 1], refs[-4:]
    experts = out.shape[0]
    rows = own_rows.shape[0]
    position = lax.axis_index("dp")
    for n, other in enumerate(others):
        wide[n] = other[...].astype(F32)
    spot = lax.broadcasted_iota(jnp.int32, (experts, experts_all), 1)
    mine = lax.broadcasted_iota(jnp.int32, (experts, experts_all), 0) + position * experts
    scales = []
    for n in range(systems):
        system = lax.rem(position - n + systems, systems)
        row = mixing[pl.ds(system, 1), :]
        column = jnp.sum(jnp.where(spot == mine, row, 0.0), axis=1, keepdims=True)
        scales.append(jnp.broadcast_to(column, (experts, LANES)))
    chunk = rows // 2
    group = max(g for g in range(1, 9) if chunk % g == 0)
    copies = []
    for part in range(2):

        def step(turn, unused, part=part):
            for n in range(group):
                at = part * chunk + turn * group + n
                total = own_rows[pl.ds(at, 1), :] * scales[0]
                for other in range(systems - 1):
                    total = total + wide[other, pl.ds(at, 1), :] * scales[other + 1]
                block[:, pl.ds(pl.multiple_of(at * LANES, LANES), LANES)] = total
            return unused

        lax.fori_loop(0, chunk // group, step, 0)
        here = slice(part * chunk * LANES, (part + 1) * chunk * LANES)
        there = slice(here.start + first_row * LANES, here.stop + first_row * LANES)
        copy = pltpu.make_async_copy(block.at[:, here], out.at[:, there], sems.at[part])
        copy.start()
        copies.append(copy)
    for copy in copies:
        copy.wait()


def spec(space=pltpu.VMEM):
    return pl.BlockSpec(memory_space=space)


KCOST = 1000


def limit(mebibytes):
    return pltpu.CompilerParams(vmem_limit_bytes=mebibytes * 1024 * 1024)


def cost(flops, size):
    return pl.CostEstimate(flops=flops, bytes_accessed=size, transcendentals=0)


def swap(x, bit):
    size = lax.axis_size("graph")
    return lax.ppermute(x, "graph", [(i, i ^ (1 << bit)) for i in range(size)])


def across(x):
    size = lax.axis_size("graph")
    pairs = [(i, i + 1) for i in range(1, size - 1, 2)]
    return lax.ppermute(x, "graph", pairs + [(j, i) for i, j in pairs])


def in_hbm(x):
    return pltpu.with_memory_space_constraint(x, pltpu.HBM)


def after(x, *others):
    return lax.optimization_barrier((x,) + others)[0]


def on_device(
    node_feats, node_cot, wigner, radial, source_atom, target_index, edge_counts,
    merged_weights, mixing,
):
    atoms, coefs, channels = node_feats.shape[1:]
    edges = source_atom.shape[1]
    size = lax.axis_size("graph")
    bits = size.bit_length() - 1
    shard_rows = merged_weights.shape[1] // LANES
    total_rows = shard_rows * size
    rows_a = (shard_rows // 2 + 7) // 8 * 8
    split = (rows_a, shard_rows - rows_a)

    feats = jnp.transpose(node_feats[0], (1, 0, 2))
    feats_far = across(feats)
    feats_core = swap(feats, 0)
    target, feats_core = lax.optimization_barrier((target_index, feats_core))

    held = pl.pallas_call(
        unroll_kernel,
        out_shape=jax.ShapeDtypeStruct((1, shard_rows, LANES), BF16),
        in_specs=[spec(pltpu.HBM)],
        out_specs=spec(),
        scratch_shapes=[
            pltpu.VMEM(merged_weights.shape, BF16),
            pltpu.VMEM((shard_rows, LANES), F32),
            pltpu.SemaphoreType.DMA,
        ],
        compiler_params=limit(6),
        cost_estimate=cost(KCOST, KCOST),
        name="rows",
    )(in_hbm(merged_weights))
    came = swap(held, bits - 1)

    hbm = spec(pltpu.HBM)
    picked_scratch = pltpu.VMEM((coefs, channels, edges), F32)
    *bmats, rot, gate, pick, feats_near = pl.pallas_call(
        cot_kernel,
        out_shape=[
            pltpu.VMEM((5 * channels, edges), BF16),
            pltpu.VMEM((4 * channels, 2 * edges), BF16),
            pltpu.VMEM((3 * channels, 2 * edges), BF16),
            pltpu.VMEM((coefs, 19, edges), F32),
            pltpu.VMEM((channels, edges), F32),
            jax.ShapeDtypeStruct((3 * atoms, edges), BF16),
            pltpu.VMEM((coefs, atoms, channels), BF16),
        ],
        in_specs=[hbm, hbm, spec(pltpu.SMEM), hbm, hbm, hbm, hbm],
        out_specs=[spec()] * 7,
        scratch_shapes=[
            pltpu.VMEM((1, edges), jnp.int32),
            pltpu.VMEM((1, edges), jnp.int32),
            pltpu.VMEM((coefs, atoms, channels), BF16),
            pltpu.VMEM((coefs, 19, edges), BF16),
            pltpu.VMEM((edges, channels), BF16),
            pltpu.SemaphoreType.DMA((6,)),
            picked_scratch,
        ],
        compiler_params=limit(12),
        cost_estimate=cost(KCOST, KCOST),
        name="cotangents",
    )(
        in_hbm(source_atom), in_hbm(target), edge_counts,
        in_hbm(jnp.transpose(node_cot[0], (1, 0, 2))), in_hbm(feats),
        in_hbm(jnp.transpose(wigner[0], (1, 0, 2))), in_hbm(radial[0]),
    )

    came = after(came, pick)
    held = jnp.concatenate([held, came], axis=0)
    held, feats_far = lax.optimization_barrier((held, feats_far))
    near, up = bits - 2, bits - 3
    pieces = {0: held, 1 << near: swap(held, near), 1 << up: swap(held, up)}

    keeps_sends = pl.pallas_call(
        grad_kernel,
        out_shape=[
            kind((2,) * (bits - 1) + (rows, LANES), dtype)
            for kind, dtype in ((pltpu.VMEM, F32), (jax.ShapeDtypeStruct, BF16))
            for rows in split
        ],
        in_specs=[spec()] * 9,
        out_specs=[spec()] * 4,
        scratch_shapes=[
            picked_scratch,
            pltpu.VMEM((5 * channels, edges), BF16),
            pltpu.VMEM((4 * channels, 2 * edges), BF16),
            pltpu.VMEM((3 * channels, 2 * edges), BF16),
            pltpu.VMEM((total_rows, LANES), F32),
        ],
        compiler_params=limit(17),
        cost_estimate=cost(KCOST, KCOST),
        name="gradients",
    )(feats_core, feats_near, feats_far, rot, gate, pick, *bmats)
    keeps, sends = keeps_sends[:2], list(keeps_sends[2:])
    *sends, pieces[1 << near], pieces[1 << up] = lax.optimization_barrier(
        (*sends, pieces[1 << near], pieces[1 << up])
    )
    pieces[1 << near | 1 << up] = swap(pieces[1 << near], up)

    low_to_high = list(range(1, bits))
    orders = [low_to_high, low_to_high[1:] + low_to_high[:1]]
    left = [list(reversed(low_to_high)) for _ in orders]

    def halve(turn, keeps, cames):
        stays, aways = [], []
        for part, (keep, came) in enumerate(zip(keeps, cames)):
            bit = orders[part][turn]
            axis = left[part].index(bit)
            left[part].remove(bit)
            shape = (2,) * len(left[part]) + came.shape[-2:]
            stay, away = pl.pallas_call(
                functools.partial(halve_kernel, axis, bit),
                out_shape=[pltpu.VMEM(shape, F32), jax.ShapeDtypeStruct(shape, BF16)],
                in_specs=[spec()] * 2,
                out_specs=[spec()] * 2,
                compiler_params=limit(6),
                cost_estimate=cost(KCOST, KCOST),
                name="halve",
            )(keep, came)
            stays.append(stay)
            aways.append(away)
        return stays, aways

    def exchange(turn, aways):
        return [swap(away, orders[part][turn]) for part, away in enumerate(aways)]

    stays, aways = halve(0, keeps, [swap(send, 0) for send in sends])

    def fan_out(some):
        some = dict(some)
        for bit in reversed(range(up)):
            some.update({mask | 1 << bit: swap(some[mask], bit) for mask in list(some)})
        return some

    last = pieces.pop(1 << near | 1 << up)
    pieces = fan_out(pieces)
    cames = exchange(0, aways)
    for turn in range(1, bits - 1):
        stays, aways = halve(turn, stays, cames)
        if turn == 1:
            masks = list(pieces)
            together = lax.optimization_barrier((*aways, *pieces.values()))
            aways, pieces = together[:2], dict(zip(masks, together[2:]))
        if turn == bits - 2:
            pieces.update(fan_out({1 << near | 1 << up: after(last, *aways)}))
        cames = exchange(turn, aways)

    masks = list(pieces)
    ready = list(pieces.values())
    grads_core, grads_own, grads_far = pl.pallas_call(
        functools.partial(backward_kernel, masks, 1 << (bits - 1)),
        out_shape=[
            jax.ShapeDtypeStruct((coefs, atoms, channels), kind) for kind in (BF16, F32, BF16)
        ],
        in_specs=[spec()] * (6 + len(masks)),
        out_specs=[spec()] * 3,
        scratch_shapes=[pltpu.VMEM((total_rows, LANES), F32)]
        + [pltpu.VMEM((g * channels, g * channels), BF16) for g in WEIGHTS]
        + [
            pltpu.VMEM((19, channels, edges), F32),
            pltpu.VMEM((coefs, channels, edges), BF16),
        ],
        compiler_params=limit(18),
        cost_estimate=cost(KCOST, KCOST),
        name="backward",
    )(*ready[: len(masks)], *bmats, rot, gate, pick)

    cames = lax.optimization_barrier((*cames, grads_own))[:2]
    systems = lax.axis_size("dp")
    shares, roundeds = [], []
    for stay, came in zip(stays, cames):
        share, rounded = pl.pallas_call(
            finish_kernel,
            out_shape=[pltpu.VMEM(came.shape, F32), jax.ShapeDtypeStruct(came.shape, BF16)],
            in_specs=[spec()] * 2,
            out_specs=[spec()] * 2,
            compiler_params=limit(6),
            cost_estimate=cost(KCOST, KCOST),
            name="finish",
        )(stay, came)
        shares.append(share)
        roundeds.append(rounded)

    from_core = swap(grads_core, 0)
    from_far = across(after(grads_far, from_core))

    own_experts = mixing.shape[1] // systems
    expert_part = None
    arrived = []
    for first_row, share, rounded in zip((0, rows_a), shares, roundeds):
        others = [
            lax.ppermute(rounded, "dp", [(i, (i + n) % systems) for i in range(systems)])
            for n in range(1, systems)
        ]
        arrived += others
        rows = share.shape[0]
        before = [] if expert_part is None else [expert_part]
        expert_part = pl.pallas_call(
            functools.partial(expert_kernel, first_row),
            out_shape=jax.ShapeDtypeStruct((own_experts, shard_rows * LANES), F32),
            in_specs=[spec()] * (1 + systems) + [spec(pl.ANY)] * len(before),
            out_specs=spec(pl.ANY),
            input_output_aliases={1 + systems: 0} if before else {},
            scratch_shapes=[
                pltpu.VMEM((max(systems - 1, 1), rows, LANES), F32),
                pltpu.VMEM((own_experts, rows * LANES), F32),
                pltpu.SemaphoreType.DMA((2,)),
            ],
            compiler_params=limit(4),
            cost_estimate=cost(KCOST, KCOST),
            name="experts",
        )(mixing, share, *others, *before)
    from_far = after(from_far, *arrived)
    total = grads_own + from_core.astype(F32) + from_far.astype(F32)
    atom_grads = jnp.transpose(total, (1, 0, 2))[None]
    return (atom_grads, expert_part)


def solution(mesh):
    in_specs = (
        P("dp", "graph", None, None),
        P("dp", "graph", None, None),
        P("dp", None, None, "graph"),
        P("dp", "graph", None),
        P("dp", "graph"),
        P("dp", "graph"),
        P("dp", "graph"),
        P("dp", "graph"),
        P(),
    )
    out_specs = (P("dp", "graph", None, None), P("dp", "graph"))
    return jax.shard_map(
        on_device, mesh=mesh, in_specs=in_specs, out_specs=out_specs, check_vma=False
    )
```
